32 devices in a mesh: parts: 2 (over x), node: 4 (over z), expert: 4 (over y, core).
Axes of the slice: x: 2, y: 2, z: 4, core: 2. Of those that a mesh axis runs over, the one named last changes fastest.
Arguments:
- hidden_in: bfloat16 [1024, 3584], P(('parts', 'node'), 'expert'), parts along dimension 0, may hold values from -6 to 6
- out_grad: bfloat16 [1024, 3584], P(('parts', 'node'), 'expert'), parts along dimension 0, may hold values from -0.59765625 to 0.59765625
- expert_ids: int32 [1024, 2], P(('parts', 'node')), parts along dimension 0, may hold values from 0 to 3, all different within a row; in each aligned block of 128 rows (0 to 127, 128 to 255, ...) at most 64 rows name the same one
- gate_weights: bfloat16 [1024, 2], P(('parts', 'node')), parts along dimension 0, may hold values from 0.099609375 to 1
- w_gate: bfloat16 [4, 2432, 3584], P('node', 'expert'), may hold values from -0.09375 to 0.09375
- w_up: bfloat16 [4, 2432, 3584], P('node', 'expert'), may hold values from -0.09375 to 0.09375
- w_down: bfloat16 [4, 2432, 3584], P('node', 'expert'), may hold values from -0.125 to 0.125
Outputs:
- grad_in: bfloat16 [1024, 3584], P(('parts', 'node'), 'expert'), parts along dimension 0
- grad_gates: float32 [1024, 2], P(('parts', 'node')), parts along dimension 0
- grad_gate: bfloat16 [8, 2432, 3584], P(('parts', 'node'), 'expert'), parts along dimension 0
- grad_up: bfloat16 [8, 2432, 3584], P(('parts', 'node'), 'expert'), parts along dimension 0
- grad_down: bfloat16 [8, 2432, 3584], P(('parts', 'node'), 'expert'), parts along dimension 0
The draws below stay inside these ranges and needn't reach their ends.
There are 2 independent parts, one for each index of `parts`. The reference program is written for one: setup_inputs(seed, part) draws one part's arguments, and reference() takes and returns one part's arrays. A program takes and returns all parts, laid end to end along the dimension named above; an argument that names none is the same for every part. Nothing has to cross between parts.
Inputs may be any that keep to these rules, and one draw needn't show every extreme that they name: `expert_ids`: each row names two different experts. Among the 128 tokens of one node group no expert is named more than 64 times, a bound that some block reaches.
All inputs are finite; a program needn't handle non-finite values.
Results may differ from the reference program's by a relative error of at most 0.0051.
Values may be sent and summed in bfloat16 or wider, within the bound.
No kernel may reach another device: no remote copies, remote signals or barrier semaphores. Data moves between devices by JAX's collectives and lax.ppermute only.
A program may use at most 128 MiB of HBM per device.

```python
import math
import jax
import jax.numpy as jnp
import numpy as np
from jax import lax

D = 3584
FF = 2432
TOK_NODE = 128
CAP = 64
EXPERTS = 4
TOKENS = 512
N_NODE = 4


def steps_of(own_key, extent, cuts, least, top_value):
    gain = 1.0
    for axis_at, blocks in cuts:
        heights = jax.random.uniform(jax.random.fold_in(jax.random.fold_in(own_key, 6), axis_at), (blocks,), jnp.float32, least / len(cuts), top_value / len(cuts))
        gain = gain * jnp.repeat(jnp.exp(heights), extent[axis_at] // blocks).reshape((-1,) + (1,) * (len(extent) - 1 - axis_at))
    return gain


def deal_out(key, own, number, rows, count, top, reach, lean):
    order = jax.random.permutation(key, count)
    packed, usual = portions_of(count, rows * top, reach, lean, True), portions_of(count, rows * top, reach, lean, False)
    places = jnp.arange(count)

    def named(tallies, offset_by):
        used = int((tallies > 0).sum())
        fixed = max(1, used // 4)
        passed = fixed + (places - fixed + offset_by * (used - fixed)) % max(1, count - fixed)
        return jnp.zeros((count,), jnp.int32).at[order[jnp.where(places < fixed, places, passed)]].set(jnp.asarray(tallies, jnp.int32))

    tallies = jnp.where(number % 4 == 0, named(packed, number // 4), named(usual, number - number // 4 - 1))
    mixed = jax.random.permutation(jax.random.fold_in(own, 3), count)
    donor, taker = mixed[0:count // 2 * 2:2], mixed[1:count // 2 * 2:2]
    slack = jnp.minimum(tallies[donor] - 1, reach - tallies[taker]) // 2
    slack = jnp.where((donor == order[0]) | (taker == order[0]) | (tallies[taker] == 0), 0, jnp.maximum(slack, 0))
    passed = jax.random.randint(jax.random.fold_in(own, 4), (count // 2,), 0, 1 << 20) % (slack + 1)
    tallies = tallies.at[donor].add(-passed).at[taker].add(passed)
    labels = jnp.searchsorted(jnp.cumsum(tallies), jnp.arange(rows * top), side="right").astype(jnp.int32)
    listing = labels.reshape(top, rows).T
    listing = listing[jax.random.permutation(jax.random.fold_in(own, 1), rows)]
    offset_by = jax.random.randint(jax.random.fold_in(own, 2), (rows, 1), 0, top)
    return jnp.take_along_axis(listing, (jnp.arange(top)[None, :] + offset_by) % top, axis=1)


def portions_of(count, total, limit, skew, full):
    loads = [(1 << 20) // math.isqrt(rank ** skew) + 1 for rank in range(1, count + 1)]
    largest = limit if full else min(limit, max(-(-total // count), total * loads[0] // sum(loads)))
    least = 1 if total - largest >= count - 1 else 0
    given, rest = [largest] + [least] * (count - 1), total - largest - least * (count - 1)
    while rest > 0:
        candidates = [i for i in range(1, count) if given[i] < largest] or [i for i in range(1, count) if given[i] < limit]
        mass, left = sum([loads[i] for i in candidates]), rest
        for i in candidates:
            addition = min(limit - given[i], max(1, left * loads[i] // mass), rest)
            given[i] = given[i] + addition
            rest = rest - addition
    return np.array(given)


def scatter_about(key, shape, deviation, limit, shards=(), kind=jnp.bfloat16):
    result = jax.random.normal(key, shape, jnp.float32) * deviation
    if len(shards) > 0:
        result = steps_of(key, shape, shards, -0.22, 0.18) * result
    return jnp.clip(result, min=-limit, max=limit).astype(kind)


def setup_inputs(seed: int = 0, part: int = 0) -> dict:
    splits = jax.random.split(jax.random.key(seed), 8)
    part_keys = jax.random.split(jax.random.fold_in(splits[7], part), 8)
    hidden_in = scatter_about(part_keys[0], (TOKENS, D), 1.0, 6.0, ((0, 4), (1, 4)))
    out_grad = scatter_about(part_keys[1], (TOKENS, D), 0.1, 0.59765625, ((0, 4), (1, 4)))
    expert_ids_keys = jax.random.split(jax.random.fold_in(part_keys[2], 1), TOKENS // TOK_NODE)
    expert_ids_turns = jax.random.permutation(jax.random.fold_in(part_keys[2], 3), TOKENS // TOK_NODE)
    expert_ids = jax.vmap(lambda own, number: deal_out(jax.random.fold_in(part_keys[2], 2), own, number, TOK_NODE, EXPERTS, 2, CAP, 2))(expert_ids_keys, expert_ids_turns).reshape((TOKENS, 2))
    gate_weights = jnp.clip(0.099609375 + 0.9003906 * jax.random.uniform(part_keys[3], (TOKENS, 2), jnp.float32) ** steps_of(part_keys[3], (TOKENS, 2), ((0, 4),), -0.2, 0.2), 0.099609375, 1.0).astype(jnp.bfloat16)
    w_gate = scatter_about(splits[4], (EXPERTS, FF, D), D ** -0.5, 0.09375, ((0, 4), (1, 4)))
    w_up = scatter_about(splits[5], (EXPERTS, FF, D), D ** -0.5, 0.09375, ((0, 4), (1, 4)))
    w_down = scatter_about(splits[6], (EXPERTS, FF, D), FF ** -0.5, 0.125, ((0, 4), (1, 4)))
    return {"hidden_in": hidden_in, "out_grad": out_grad, "expert_ids": expert_ids, "gate_weights": gate_weights, "w_gate": w_gate, "w_up": w_up, "w_down": w_down}


def contract_rows(left, right):
    return lax.dot_general(left, right, (((0,), (0,)), ((), ())), preferred_element_type=jnp.float32)


def contract_cols(left, right):
    return lax.dot_general(left, right, (((1,), (1,)), ((), ())), preferred_element_type=jnp.float32)


def expert_backward(rows_in, rows_grad, row_weight, gate_mat, up_mat, down_mat):
    gate_pre = contract_cols(rows_in, gate_mat)
    up_pre = contract_cols(rows_in, up_mat)
    sigmoid_gate = jax.nn.sigmoid(gate_pre)
    silu_gate = gate_pre * sigmoid_gate
    hidden = silu_gate * up_pre
    back_hidden = contract_cols(rows_grad, down_mat)
    statistic = jnp.sum(hidden * back_hidden, axis=1)
    scaled = row_weight[:, None] * back_hidden
    grad_gate_pre = (scaled * up_pre * sigmoid_gate * (1.0 + gate_pre * (1.0 - sigmoid_gate))).astype(jnp.bfloat16)
    grad_up_pre = (scaled * silu_gate).astype(jnp.bfloat16)
    weighted_hidden = (row_weight[:, None] * hidden).astype(jnp.bfloat16)
    grad_down = contract_rows(weighted_hidden, rows_grad).astype(jnp.bfloat16)
    grad_gate = contract_rows(grad_gate_pre, rows_in).astype(jnp.bfloat16)
    grad_up = contract_rows(grad_up_pre, rows_in).astype(jnp.bfloat16)
    input_part = (jnp.dot(grad_gate_pre, gate_mat, preferred_element_type=jnp.float32)
                  + jnp.dot(grad_up_pre, up_mat, preferred_element_type=jnp.float32))
    return grad_gate, grad_up, grad_down, input_part, statistic


def reference(hidden_in, out_grad, expert_ids, gate_weights, w_gate, w_up, w_down):
    count_tok = hidden_in.shape[0]
    pad_in = jnp.concatenate([hidden_in, jnp.zeros((1, D), hidden_in.dtype)], axis=0)
    pad_grad = jnp.concatenate([out_grad, jnp.zeros((1, D), out_grad.dtype)], axis=0)
    weights_full = gate_weights.astype(jnp.float32)

    def per_expert(expert_id):
        member = expert_ids == expert_id
        row_weight = jnp.sum(jnp.where(member, weights_full, jnp.float32(0.0)), axis=1)
        chosen = jnp.any(member, axis=1)
        index = jnp.nonzero(chosen, size=N_NODE * CAP, fill_value=count_tok)[0].astype(jnp.int32)
        pad_weight = jnp.concatenate([row_weight, jnp.zeros((1,), jnp.float32)])
        results = expert_backward(pad_in[index], pad_grad[index], pad_weight[index],
                                  w_gate[expert_id], w_up[expert_id], w_down[expert_id])
        return results + (index,)

    grad_gate, grad_up, grad_down, input_parts, statistics, indices = lax.map(
        per_expert, jnp.arange(EXPERTS, dtype=jnp.int32))
    flat_index = indices.reshape(-1)
    grad_total = jnp.zeros((count_tok + 1, D), jnp.float32).at[flat_index].add(input_parts.reshape(-1, D))
    table = jnp.zeros((EXPERTS, count_tok + 1), jnp.float32).at[
        jnp.arange(EXPERTS, dtype=jnp.int32)[:, None], indices].set(statistics)
    grad_gates = table[expert_ids, jnp.arange(count_tok, dtype=jnp.int32)[:, None]]
    grad_in = grad_total[:count_tok].astype(jnp.bfloat16)
    return grad_in, grad_gates, grad_gate, grad_up, grad_down
```

```python
import functools

import jax
import jax.numpy as jnp
from jax import lax
from jax.experimental import pallas as pl
from jax.experimental.pallas import tpu as pltpu
from jax.sharding import PartitionSpec as P

BF16 = jnp.bfloat16
F32 = jnp.float32


def dot_nt(left, right):
    return lax.dot_general(left, right, (((1,), (1,)), ((), ())), preferred_element_type=F32)


def dot_tn(left, right):
    return lax.dot_general(left, right, (((0,), (0,)), ((), ())), preferred_element_type=F32)


def dot_nn(left, right):
    return lax.dot_general(left, right, (((1,), (0,)), ((), ())), preferred_element_type=F32)


def call(kernel, outs, *args, flops=0, nbytes=0, vmem=24 << 20, scratch=(), fast=()):
    args = [
        pltpu.with_memory_space_constraint(a, pltpu.VMEM) if i in fast else a
        for i, a in enumerate(args)
    ]
    return pl.pallas_call(
        kernel,
        out_shape=outs,
        in_specs=[pl.BlockSpec(memory_space=pltpu.VMEM)] * len(args),
        out_specs=[pl.BlockSpec(memory_space=pltpu.VMEM)] * len(outs),
        scratch_shapes=list(scratch),
        compiler_params=pltpu.CompilerParams(vmem_limit_bytes=vmem),
        cost_estimate=pl.CostEstimate(flops=flops, bytes_accessed=nbytes, transcendentals=0),
    )(*args)


def slots_of(ids, expert, capacity):
    tokens = ids.shape[1]
    routed = jnp.max((ids == expert).astype(F32), axis=0, keepdims=True)
    before = (
        lax.broadcasted_iota(jnp.int32, (tokens, tokens), 0)
        < lax.broadcasted_iota(jnp.int32, (tokens, tokens), 1)
    ).astype(BF16)
    position = dot_nn(jnp.broadcast_to(routed, (8, tokens)).astype(BF16), before)[0:1]
    slot = lax.broadcasted_iota(jnp.int32, (capacity, tokens), 0).astype(F32)
    return jnp.where((slot == position) & (routed > 0.0), 1.0, 0.0)


def pack_kernel(groups, ids_ref, gates_ref, hidden_ref, grad_ref, *outs):
    me = lax.axis_index("node")
    ids = ids_ref[...]
    gates = gates_ref[...].astype(F32)
    capacity = ids.shape[1] // 2
    for shift in range(groups):
        expert = me ^ shift
        chosen = slots_of(ids, expert, capacity)
        one_hot = chosen.astype(BF16)
        in_ref, grad_out, weight_ref = outs[3 * shift : 3 * shift + 3]
        in_ref[...] = dot_nn(one_hot, hidden_ref[...]).astype(BF16)
        grad_out[...] = dot_nn(one_hot, grad_ref[...]).astype(BF16)
        weight = jnp.sum(jnp.where(ids == expert, gates, 0.0), axis=0, keepdims=True)
        weight_ref[...] = dot_nt(jnp.broadcast_to(weight, (16, ids.shape[1])).astype(BF16), one_hot).astype(BF16)


def assemble(parts, groups, rows_ref):
    me = lax.axis_index("expert")
    capacity, width = parts[0].shape
    for index, part in enumerate(parts):
        relative, shift = divmod(index, groups)
        start = pl.multiple_of((me ^ relative) * width, width)
        rows_ref[shift * capacity : (shift + 1) * capacity, pl.ds(start, width)] = part[...]


def front_kernel(groups, *refs):
    parts = refs[: 4 * groups]
    gate_w, up_w, rows_ref, gate_ref, up_ref = refs[4 * groups :]
    assemble(parts, groups, rows_ref)
    rows = rows_ref[...]
    gate_ref[...] = dot_nt(gate_w[0], rows)
    up_ref[...] = dot_nt(up_w[0], rows)


def middle_kernel(groups, *refs):
    parts = refs[: 4 * groups]
    weights = refs[4 * groups : 5 * groups]
    down_w, gate_ref, up_ref, rows_ref, dgate_ref, dup_ref, hid_ref, stat_ref = refs[5 * groups :]
    assemble(parts, groups, rows_ref)
    back = dot_nt(down_w[0], rows_ref[...])
    weight = jnp.concatenate([w[0:1, :] for w in weights], axis=1).astype(F32)
    gate = gate_ref[...]
    up = up_ref[...]
    sig = 1.0 / (1.0 + jnp.exp(-gate))
    silu = gate * sig
    hidden = silu * up
    stat_ref[...] = jnp.broadcast_to(jnp.sum(hidden * back, axis=0, keepdims=True), stat_ref.shape)
    scaled = weight * back
    dgate_ref[...] = (scaled * up * sig * (1.0 + gate * (1.0 - sig))).astype(BF16)
    dup_ref[...] = (scaled * silu).astype(BF16)
    hid_ref[...] = (weight * hidden).astype(BF16)


def input_kernel(far, dgate_ref, dup_ref, gate_w, up_w, keep_ref, give_ref):
    me = lax.axis_index("expert")
    width = keep_ref.shape[1]
    dgate = dgate_ref[...].T
    dup = dup_ref[...].T
    for ref, relative in ((give_ref, far + 1), (keep_ref, far)):
        columns = pl.ds(pl.multiple_of((me ^ relative) * width, width), width)
        total = dot_nn(dgate, gate_w[0, :, columns]) + dot_nn(dup, up_w[0, :, columns])
        ref[...] = total.astype(ref.dtype)


def add_kernel(groups, left, right, *outs):
    capacity = outs[0].shape[0]
    for shift in range(groups):
        rows = slice(shift * capacity, (shift + 1) * capacity)
        outs[shift][...] = (left[rows].astype(F32) + right[rows].astype(F32)).astype(BF16)


def join_kernel(left, right, third, out):
    out[...] = (left[...].astype(F32) + right[...].astype(F32) + third[...].astype(F32)).astype(BF16)


def grad_kernel(left_ref, rows_ref, out_ref):
    tile = 512
    def step(i, _):
        columns = pl.ds(pl.multiple_of(i * tile, tile), tile)
        out_ref[0, :, columns] = dot_nn(left_ref[...], rows_ref[:, columns]).astype(BF16)
        return _
    lax.fori_loop(0, rows_ref.shape[1] // tile, step, 0)


def finish_kernel(groups, ids_ref, stat_ref, *refs):
    parts = refs[:groups]
    grad_ref, gates_ref = refs[groups:]
    me = lax.axis_index("node")
    ids = ids_ref[...]
    capacity = ids.shape[1] // 2
    total = jnp.zeros(grad_ref.shape, F32)
    gates = jnp.zeros(ids.shape, F32)
    for shift in range(groups):
        expert = me ^ shift
        chosen = slots_of(ids, expert, capacity)
        total = total + dot_tn(chosen.astype(BF16), parts[shift][...])
        stat = jnp.broadcast_to(stat_ref[shift : shift + 1], (8, capacity))
        spread = lax.dot_general(
            stat, chosen, (((1,), (0,)), ((), ())),
            precision=lax.Precision.HIGHEST, preferred_element_type=F32,
        )[0:1]
        gates = gates + jnp.where(ids == expert, spread, 0.0)
    grad_ref[...] = total.astype(BF16)
    gates_ref[...] = gates


def fast_local(hidden_in, out_grad, expert_ids, gate_weights, w_gate, w_up, w_down):
    groups = lax.axis_size("node")
    experts = lax.axis_size("expert")
    tokens, width = hidden_in.shape
    capacity = tokens // 2
    rows = groups * capacity
    units, features = w_gate.shape[1:]
    shape = jax.ShapeDtypeStruct

    def over_node(x, shift):
        return lax.ppermute(x, "node", [(i, i ^ shift) for i in range(groups)])

    def over_expert(x, relative):
        return lax.ppermute(x, "expert", [(i, i ^ relative) for i in range(experts)])

    ids = expert_ids.T
    packed = call(
        functools.partial(pack_kernel, groups),
        [shape((capacity, width), BF16), shape((capacity, width), BF16), shape((16, capacity), BF16)] * groups,
        ids, gate_weights.T, hidden_in, out_grad,
        flops=4 * rows * tokens * width, nbytes=6 * tokens * width,
    )

    def spread(blocks):
        own = [blocks[0]] + [over_node(blocks[s], s) for s in range(1, groups)]
        other = [over_expert(x, 2) for x in own]
        partner = [over_expert(x, 1) for x in own]
        across = [over_expert(x, 1) for x in other]
        return own + partner + other + across

    ins = spread(packed[0::3])
    grads = spread(packed[1::3])
    weights = [packed[2]] + [over_node(packed[3 * s + 2], s) for s in range(1, groups)]

    dense = 2 * rows * units * features
    rows_in, gate, up = call(
        functools.partial(front_kernel, groups),
        [shape((rows, features), BF16), shape((units, rows), F32), shape((units, rows), F32)],
        *ins, w_gate, w_up, flops=2 * dense, nbytes=4 * units * features,
    )
    rows_grad, dgate, dup, hid, stat = call(
        functools.partial(middle_kernel, groups),
        [shape((rows, features), BF16)] + [shape((units, rows), BF16)] * 3 + [shape((8, rows), F32)],
        *grads, *weights, w_down, gate, up, flops=dense, nbytes=2 * units * features,
    )
    far_keep, far_give = call(
        functools.partial(input_kernel, 2),
        [shape((rows, width), BF16)] * 2,
        dgate, dup, w_gate, w_up, flops=dense, nbytes=2 * units * features,
    )
    far_got = over_expert(far_give, 1)
    near_keep, near_give = call(
        functools.partial(input_kernel, 0),
        [shape((rows, width), BF16)] * 2,
        dgate, dup, w_gate, w_up, flops=dense, nbytes=2 * units * features,
    )
    near_got = over_expert(near_give, 1)
    far_sum = call(functools.partial(add_kernel, groups), [shape((capacity, width), BF16)] * groups, far_keep, far_got,
                   nbytes=6 * rows * width)
    crossed = [over_expert(x, 2) for x in far_sum]
    back = []
    for s in range(groups):
        block = slice(s * capacity, (s + 1) * capacity)
        total = call(join_kernel, [shape((capacity, width), BF16)], near_keep[block], near_got[block], crossed[s])[0]
        back.append(over_node(total, s) if s else total)

    stat_rows = stat[0].reshape(groups, capacity)
    stat_pair = stat_rows + over_expert(stat_rows, 1)
    stat_total = stat_pair + over_expert(stat_pair, 2)
    stat_back = jnp.concatenate(
        [stat_total[0:1]] + [over_node(stat_total[s : s + 1], s) for s in range(1, groups)], axis=0
    )

    weight_grads = [
        call(grad_kernel, [shape((1, units, features), BF16)], left, right, flops=dense, nbytes=2 * units * features)[0]
        for left, right in ((dgate, rows_in), (dup, rows_in), (hid, rows_grad))
    ]
    grad_in, grad_gates = call(
        functools.partial(finish_kernel, groups),
        [shape((tokens, width), BF16), shape(ids.shape, F32)],
        ids, stat_back, *back,
    )
    return (grad_in, grad_gates.T, *weight_grads)


def contract_rows(left, right):
    return lax.dot_general(
        left, right, (((0,), (0,)), ((), ())), preferred_element_type=jnp.float32
    )


def contract_cols(left, right):
    return lax.dot_general(
        left, right, (((1,), (1,)), ((), ())), preferred_element_type=jnp.float32
    )


def expert_backward(rows_in, rows_grad, row_weight, gate_mat, up_mat, down_mat):
    gate_pre = contract_cols(rows_in, gate_mat)
    up_pre = contract_cols(rows_in, up_mat)
    sigmoid_gate = jax.nn.sigmoid(gate_pre)
    silu_gate = gate_pre * sigmoid_gate
    hidden = silu_gate * up_pre
    back_hidden = contract_cols(rows_grad, down_mat)
    statistic = jnp.sum(hidden * back_hidden, axis=1)
    scaled = row_weight[:, None] * back_hidden
    grad_gate_pre = (
        scaled * up_pre * sigmoid_gate * (1.0 + gate_pre * (1.0 - sigmoid_gate))
    ).astype(jnp.bfloat16)
    grad_up_pre = (scaled * silu_gate).astype(jnp.bfloat16)
    weighted_hidden = (row_weight[:, None] * hidden).astype(jnp.bfloat16)
    grad_down = contract_rows(weighted_hidden, rows_grad).astype(jnp.bfloat16)
    grad_gate = contract_rows(grad_gate_pre, rows_in).astype(jnp.bfloat16)
    grad_up = contract_rows(grad_up_pre, rows_in).astype(jnp.bfloat16)
    return (grad_gate, grad_up, grad_down, grad_gate_pre, grad_up_pre, statistic)


def general_local(hidden_in, out_grad, expert_ids, gate_weights, w_gate, w_up, w_down):
    groups = lax.axis_size("node")
    count_tok = hidden_in.shape[0]
    capacity = count_tok // 2
    group_ids = jnp.arange(groups, dtype=jnp.int32)
    member = expert_ids[:, :, None] == group_ids[None, None, :]
    routed = jnp.any(member, axis=1)
    routed_int = routed.astype(jnp.int32)
    position = jnp.cumsum(routed_int, axis=0) - routed_int
    weight_of = jnp.sum(
        jnp.where(member, gate_weights[:, :, None].astype(jnp.float32), jnp.float32(0.0)), axis=1
    )
    slot_ids = jnp.arange(capacity, dtype=jnp.int32)
    landing = routed[:, :, None] & (position[:, :, None] == slot_ids[None, None, :])
    token_of = jnp.sum(
        jnp.where(landing, jnp.arange(count_tok, dtype=jnp.int32)[:, None, None], 0), axis=0
    )
    filled = jnp.any(landing, axis=0)
    send_weight = jnp.where(
        filled, weight_of[token_of, group_ids[:, None]], jnp.float32(0.0)
    ).astype(jnp.bfloat16)

    def pack_rows(source):
        return jnp.where(filled[:, :, None], source[token_of], jnp.zeros((), source.dtype))

    slice_in, slice_grad, recv_weight = (
        lax.all_to_all(pack_rows(hidden_in), "node", split_axis=0, concat_axis=0, tiled=True),
        lax.all_to_all(pack_rows(out_grad), "node", split_axis=0, concat_axis=0, tiled=True),
        lax.all_to_all(send_weight, "node", split_axis=0, concat_axis=0, tiled=True),
    )
    rows_in, rows_grad = (
        lax.all_gather(slice_in, "expert", axis=2, tiled=True),
        lax.all_gather(slice_grad, "expert", axis=2, tiled=True),
    )
    total_rows = groups * capacity
    features = rows_in.shape[2]
    row_weight = recv_weight.reshape(total_rows).astype(jnp.float32)
    gate_mat = w_gate[0]
    up_mat = w_up[0]
    grad_gate, grad_up, grad_down, grad_gate_pre, grad_up_pre, statistic = expert_backward(
        rows_in.reshape(total_rows, features),
        rows_grad.reshape(total_rows, features),
        row_weight,
        gate_mat,
        up_mat,
        w_down[0],
    )
    input_part = jnp.dot(grad_gate_pre, gate_mat, preferred_element_type=jnp.float32) + jnp.dot(
        grad_up_pre, up_mat, preferred_element_type=jnp.float32
    )
    input_slice = lax.psum_scatter(input_part, "expert", scatter_dimension=1, tiled=True)
    stat_total = lax.psum(statistic, "expert")
    slice_width = input_slice.shape[1]
    back_input, back_stat = (
        lax.all_to_all(
            input_slice.reshape(groups, capacity, slice_width),
            "node",
            split_axis=0,
            concat_axis=0,
            tiled=True,
        ),
        lax.all_to_all(
            stat_total.reshape(groups, capacity), "node", split_axis=0, concat_axis=0, tiled=True
        ),
    )
    flat_input = back_input.reshape(total_rows, slice_width)
    flat_stat = back_stat.reshape(total_rows)
    flat_index = expert_ids * capacity + jnp.take_along_axis(position, expert_ids, axis=1)
    grad_in = (flat_input[flat_index[:, 0]] + flat_input[flat_index[:, 1]]).astype(jnp.bfloat16)
    grad_gates = flat_stat[flat_index]
    return (grad_in, grad_gates, grad_gate[None], grad_up[None], grad_down[None])


def local(hidden_in, *rest):
    if lax.axis_size("expert") == 4 and hidden_in.shape[1] % 128 == 0:
        return fast_local(hidden_in, *rest)
    return general_local(hidden_in, *rest)


def solution(mesh):
    return jax.shard_map(
        local,
        mesh=mesh,
        in_specs=(
            P(("parts", "node"), "expert"),
            P(("parts", "node"), "expert"),
            P(("parts", "node"), None),
            P(("parts", "node"), None),
            P("node", "expert", None),
            P("node", "expert", None),
            P("node", "expert", None),
        ),
        out_specs=(
            P(("parts", "node"), "expert"),
            P(("parts", "node"), None),
            P(("parts", "node"), "expert", None),
            P(("parts", "node"), "expert", None),
            P(("parts", "node"), "expert", None),
        ),
        check_vma=False,
    )
```

```python
import functools

import jax
import jax.numpy as jnp
from jax import lax
from jax.experimental import pallas as pl
from jax.experimental.pallas import tpu as pltpu
from jax.sharding import PartitionSpec as P

BF16 = jnp.bfloat16
F32 = jnp.float32
MIB = 1 << 20


def dot_nt(left, right):
    return lax.dot_general(left, right, (((1,), (1,)), ((), ())), preferred_element_type=F32)


def dot_tn(left, right):
    return lax.dot_general(left, right, (((0,), (0,)), ((), ())), preferred_element_type=F32)


def dot_nn(left, right):
    return lax.dot_general(left, right, (((1,), (0,)), ((), ())), preferred_element_type=F32)


def call(kernel, outs, *args, flops=0, nbytes=0, vmem=6 * MIB, scratch=(), in_hbm=()):
    args = [
        pltpu.with_memory_space_constraint(a, pltpu.HBM) if i in in_hbm else a for i, a in enumerate(args)
    ]
    return pl.pallas_call(
        kernel,
        out_shape=outs,
        in_specs=[
            pl.BlockSpec(memory_space=pltpu.HBM if i in in_hbm else pltpu.VMEM) for i in range(len(args))
        ],
        out_specs=[pl.BlockSpec(memory_space=pltpu.VMEM)] * len(outs),
        scratch_shapes=list(scratch),
        compiler_params=pltpu.CompilerParams(vmem_limit_bytes=vmem),
        cost_estimate=pl.CostEstimate(flops=flops, bytes_accessed=nbytes, transcendentals=0),
    )(*args)


def slots_of(ids, expert, capacity):
    tokens = ids.shape[1]
    routed = jnp.max((ids == expert).astype(F32), axis=0, keepdims=True)
    before = (
        lax.broadcasted_iota(jnp.int32, (tokens, tokens), 0)
        < lax.broadcasted_iota(jnp.int32, (tokens, tokens), 1)
    ).astype(BF16)
    position = dot_nn(jnp.broadcast_to(routed, (8, tokens)).astype(BF16), before)[0:1]
    slot = lax.broadcasted_iota(jnp.int32, (capacity, tokens), 0).astype(F32)
    return jnp.where((slot == position) & (routed > 0.0), 1.0, 0.0)


def pack_kernel(groups, *refs):
    sources, outs, local, sems = refs[:4], refs[4 : 4 + groups], refs[4 + groups : 8 + groups], refs[-1]
    copies = [pltpu.make_async_copy(a, b, sems.at[i]) for i, (a, b) in enumerate(zip(sources, local))]
    for copy in copies:
        copy.start()
    ids_ref, gates_ref, hidden_ref, grad_ref = local
    me = lax.axis_index("node")
    copies[0].wait()
    copies[1].wait()
    ids = ids_ref[...]
    capacity = ids.shape[1] // 2
    one_hots = [slots_of(ids, me ^ shift, capacity) for shift in range(groups)]
    copies[2].wait()
    for one_hot, out in zip(one_hots, outs):
        out[:capacity] = dot_nn(one_hot.astype(BF16), hidden_ref[...]).astype(BF16)
    gates = gates_ref[...].astype(F32)
    copies[3].wait()
    for shift, (one_hot, out) in enumerate(zip(one_hots, outs)):
        weight = jnp.sum(jnp.where(ids == (me ^ shift), gates, 0.0), axis=0, keepdims=True)
        out[capacity:] = dot_nn((one_hot * weight).astype(BF16), grad_ref[...]).astype(BF16)


def load_kernel(*refs):
    count = len(refs) // 2
    sources, outs, sems = refs[:count], refs[count : 2 * count], refs[-1]
    copies = [pltpu.make_async_copy(a, b, sems.at[i]) for i, (a, b) in enumerate(zip(sources, outs))]
    for copy in copies:
        copy.start()
    for copy in copies:
        copy.wait()


def assemble(parts, relatives, groups, base, rows_ref, grads_ref):
    me = lax.axis_index("expert")
    capacity, width = parts[0].shape[0] // 2, parts[0].shape[1]
    for index, part in enumerate(parts):
        place, shift = divmod(index, groups)
        columns = pl.ds(pl.multiple_of(((me ^ relatives[place]) - base) * width, width), width)
        rows = slice(shift * capacity, (shift + 1) * capacity)
        rows_ref[rows, columns] = part[:capacity]
        grads_ref[rows, columns] = part[capacity:]


def local_kernel(groups, *refs):
    parts = refs[: 2 * groups]
    gate_w, up_w, down_w, gate_ref, up_ref, back_ref, rows_ref, grads_ref = refs[2 * groups :]
    base = (lax.axis_index("expert") // 2) * 2
    assemble(parts, (0, 1), groups, base, rows_ref, grads_ref)
    half = rows_ref.shape[1]
    columns = pl.ds(pl.multiple_of(base * (half // 2), half), half)
    gate_ref[...] = dot_nt(gate_w[0, :, columns], rows_ref[...])
    up_ref[...] = dot_nt(up_w[0, :, columns], rows_ref[...])
    back_ref[...] = dot_nt(down_w[0, :, columns], grads_ref[...])


def middle_kernel(groups, *refs):
    parts = refs[: 4 * groups]
    (gate_w, up_w, down_w, gate_ref, up_ref, back_ref,
     rows_ref, grads_ref, dgate_ref, dup_ref, hid_ref, stat_ref) = refs[4 * groups :]
    assemble(parts, (2, 3, 0, 1), groups, 0, rows_ref, grads_ref)
    half = rows_ref.shape[1] // 2
    columns = pl.ds(pl.multiple_of((1 - lax.axis_index("expert") // 2) * half, half), half)
    gate = gate_ref[...] + dot_nt(gate_w[0, :, columns], rows_ref[:, columns])
    up = up_ref[...] + dot_nt(up_w[0, :, columns], rows_ref[:, columns])
    back = back_ref[...] + dot_nt(down_w[0, :, columns], grads_ref[:, columns])
    sig = 1.0 / (1.0 + jnp.exp(-gate))
    silu = gate * sig
    hidden = silu * up
    stat_ref[...] = jnp.broadcast_to(jnp.sum(hidden * back, axis=0, keepdims=True), stat_ref.shape)
    dgate_ref[...] = (back * up * sig * (1.0 + gate * (1.0 - sig))).astype(BF16)
    dup_ref[...] = (back * silu).astype(BF16)
    hid_ref[...] = hidden.astype(BF16)


EXTRA = 8


def halves_of(row):
    high = row.astype(BF16).astype(F32)
    index = lax.broadcasted_iota(jnp.int32, (EXTRA, row.shape[1]), 0)
    return jnp.where(index == 0, high, jnp.where(index == 1, row - high, 0.0)).astype(BF16)


def row_of(halves):
    return halves[0:1].astype(F32) + halves[1:2].astype(F32)


def input_kernel(far, dgate_ref, dup_ref, gate_w, up_w, stat_ref, give_ref, keep_ref):
    me = lax.axis_index("expert")
    rows, width = keep_ref.shape
    dgate = dgate_ref[...].T
    dup = dup_ref[...].T
    for ref, relative in ((give_ref, far + 1), (keep_ref, far)):
        columns = pl.ds(pl.multiple_of((me ^ relative) * width, width), width)
        total = dot_nn(dgate, gate_w[0, :, columns]) + dot_nn(dup, up_w[0, :, columns])
        ref[:rows] = total.astype(ref.dtype)
    if far:
        give_ref[rows:, :rows] = halves_of(stat_ref[0:1])
        give_ref[rows:, rows:] = jnp.zeros((EXTRA, width - rows), BF16)


def add_kernel(groups, keep, got, stat_ref, *outs):
    capacity = outs[0].shape[0] - EXTRA
    rows = groups * capacity
    stat = stat_ref[0:1] + row_of(got[rows:, :rows])
    outs[groups][...] = jnp.broadcast_to(stat, outs[groups].shape)
    for shift in range(groups):
        block = slice(shift * capacity, (shift + 1) * capacity)
        outs[shift][:capacity] = (keep[block] + got[block].astype(F32)).astype(BF16)
        outs[shift][capacity:, :capacity] = halves_of(stat[:, block])
        outs[shift][capacity:, capacity:] = jnp.zeros((EXTRA, outs[shift].shape[1] - capacity), BF16)


def join_kernel(shift, keep, got, crossed, stat_ref, out):
    capacity = out.shape[0] - EXTRA
    block = slice(shift * capacity, (shift + 1) * capacity)
    out[:capacity] = (keep[block] + got[block].astype(F32) + crossed[:capacity].astype(F32)).astype(BF16)
    out[capacity:, :capacity] = halves_of(stat_ref[0:1, block] + row_of(crossed[capacity:, :capacity]))
    out[capacity:, capacity:] = jnp.zeros((EXTRA, out.shape[1] - capacity), BF16)


def grad_kernel(left_ref, rows_ref, out_ref):
    out_ref[0] = dot_nn(left_ref[...], rows_ref[...]).astype(BF16)


def weight_grad(left, rows):
    units, count = left.shape
    features = rows.shape[1]
    tile = 512 if features % 512 == 0 else features
    return pl.pallas_call(
        grad_kernel,
        out_shape=jax.ShapeDtypeStruct((1, units, features), BF16),
        grid=(features // tile,),
        in_specs=[
            pl.BlockSpec((units, count), lambda i: (0, 0)),
            pl.BlockSpec((count, tile), lambda i: (0, i)),
        ],
        out_specs=pl.BlockSpec((1, units, tile), lambda i: (0, 0, i)),
        compiler_params=pltpu.CompilerParams(vmem_limit_bytes=8 * MIB),
        cost_estimate=pl.CostEstimate(flops=0, bytes_accessed=0, transcendentals=0),
    )(left, rows)


def finish_kernel(groups, ids_ref, gates_in_ref, *refs):
    parts = refs[:groups]
    grad_ref, gates_ref = refs[groups:]
    me = lax.axis_index("node")
    ids = ids_ref[...]
    capacity = ids.shape[1] // 2
    total = jnp.zeros(grad_ref.shape, F32)
    gates = jnp.zeros(ids.shape, F32)
    for shift in range(groups):
        expert = me ^ shift
        chosen = slots_of(ids, expert, capacity)
        total = total + dot_tn(chosen.astype(BF16), parts[shift][:capacity])
        halves = dot_nn(parts[shift][capacity:, :capacity], chosen.astype(BF16))
        gates = gates + jnp.where(ids == expert, halves[0:1] + halves[1:2], 0.0)
    grad_ref[...] = total.astype(BF16)
    gates_ref[...] = gates / gates_in_ref[...].astype(F32)


def fast_local(hidden_in, out_grad, expert_ids, gate_weights, w_gate, w_up, w_down):
    groups = lax.axis_size("node")
    experts = lax.axis_size("expert")
    tokens, width = hidden_in.shape
    capacity = tokens // 2
    rows = groups * capacity
    units, features = w_gate.shape[1:]
    shape = jax.ShapeDtypeStruct
    after = lax.optimization_barrier

    def over_node(x, shift):
        return lax.ppermute(x, "node", [(i, i ^ shift) for i in range(groups)])

    def over_expert(x, relative):
        return lax.ppermute(x, "expert", [(i, i ^ relative) for i in range(experts)])

    ids, gates = expert_ids.T, gate_weights.T
    blocks = call(
        functools.partial(pack_kernel, groups),
        [shape((tokens, width), BF16)] * groups,
        ids, gates, hidden_in, out_grad,
        flops=4 * rows * tokens * width, nbytes=6 * tokens * width, in_hbm=(0, 1, 2, 3),
        scratch=[
            pltpu.VMEM(ids.shape, ids.dtype), pltpu.VMEM(gates.shape, gates.dtype),
            pltpu.VMEM((tokens, width), BF16), pltpu.VMEM((tokens, width), BF16), pltpu.SemaphoreType.DMA((4,)),
        ],
    )
    own = [blocks[0]] + [over_node(blocks[s], s) for s in range(1, groups)]
    partner = [over_expert(x, 1) for x in own]
    mats = after((w_gate, w_up, w_down, own[1]))[:3]
    mats = call(load_kernel, [shape(m.shape, BF16) for m in mats], *mats, nbytes=12 * units * features,
                in_hbm=(0, 1, 2), scratch=[pltpu.SemaphoreType.DMA((3,))])
    other = [over_expert(own[0], 2)]
    other.append(over_expert(own[1], 2))
    for s in range(2, groups):
        other.append(over_expert(after((own[s], other[1], mats[0]))[0], 2))
    across = [over_expert(x, 1) for x in other]

    dense = 2 * rows * units * features
    partial_sums = call(
        functools.partial(local_kernel, groups),
        [shape((units, rows), F32)] * 3,
        *own, *partner, *mats, flops=3 * dense // 2, nbytes=3 * units * features,
        scratch=[pltpu.VMEM((rows, 2 * width), BF16)] * 2,
    )
    rows_in, rows_grad, dgate, dup, hid, stat = call(
        functools.partial(middle_kernel, groups),
        [shape((rows, features), BF16)] * 2 + [shape((units, rows), BF16)] * 3 + [shape((8, rows), F32)],
        *other, *across, *own, *partner, *mats, *partial_sums,
        flops=3 * dense // 2, nbytes=3 * units * features,
    )

    def input_part(far):
        return call(
            functools.partial(input_kernel, far),
            [shape((rows + (EXTRA if far else 0), width), BF16), shape((rows, width), F32)],
            dgate, dup, mats[0], mats[1], stat, flops=dense, nbytes=2 * units * features,
        )

    far_give, far_keep = input_part(2)
    far_got = over_expert(far_give, 1)
    near_give, near_keep = input_part(0)
    near_got = over_expert(near_give, 1)
    *far_sum, stat_pair = call(
        functools.partial(add_kernel, groups),
        [shape((capacity + EXTRA, width), BF16)] * groups + [shape((8, rows), F32)],
        far_keep, far_got, stat, nbytes=6 * rows * width,
    )
    back, totals = [None] * groups, []
    for s in reversed(range(groups)):
        totals += call(functools.partial(join_kernel, s), [shape((capacity + EXTRA, width), BF16)],
                       near_keep, near_got, over_expert(far_sum[s], 2), stat_pair)
        back[s] = over_node(totals[-1], s) if s else totals[-1]

    dgate, dup, hid, _ = after((dgate, dup, hid, tuple(totals[:-1])))
    weight_grads = [weight_grad(dgate, rows_in), weight_grad(dup, rows_in), weight_grad(hid, rows_grad)]

    grad_in, grad_gates = call(
        functools.partial(finish_kernel, groups),
        [shape((tokens, width), BF16), shape(ids.shape, F32)],
        ids, gates, *back,
    )
    return (grad_in, grad_gates.T, *weight_grads)


def contract_rows(left, right):
    return lax.dot_general(
        left, right, (((0,), (0,)), ((), ())), preferred_element_type=jnp.float32
    )


def contract_cols(left, right):
    return lax.dot_general(
        left, right, (((1,), (1,)), ((), ())), preferred_element_type=jnp.float32
    )


def expert_backward(rows_in, rows_grad, row_weight, gate_mat, up_mat, down_mat):
    gate_pre = contract_cols(rows_in, gate_mat)
    up_pre = contract_cols(rows_in, up_mat)
    sigmoid_gate = jax.nn.sigmoid(gate_pre)
    silu_gate = gate_pre * sigmoid_gate
    hidden = silu_gate * up_pre
    back_hidden = contract_cols(rows_grad, down_mat)
    statistic = jnp.sum(hidden * back_hidden, axis=1)
    scaled = row_weight[:, None] * back_hidden
    grad_gate_pre = (
        scaled * up_pre * sigmoid_gate * (1.0 + gate_pre * (1.0 - sigmoid_gate))
    ).astype(jnp.bfloat16)
    grad_up_pre = (scaled * silu_gate).astype(jnp.bfloat16)
    weighted_hidden = (row_weight[:, None] * hidden).astype(jnp.bfloat16)
    grad_down = contract_rows(weighted_hidden, rows_grad).astype(jnp.bfloat16)
    grad_gate = contract_rows(grad_gate_pre, rows_in).astype(jnp.bfloat16)
    grad_up = contract_rows(grad_up_pre, rows_in).astype(jnp.bfloat16)
    return (grad_gate, grad_up, grad_down, grad_gate_pre, grad_up_pre, statistic)


def general_local(hidden_in, out_grad, expert_ids, gate_weights, w_gate, w_up, w_down):
    groups = lax.axis_size("node")
    count_tok = hidden_in.shape[0]
    capacity = count_tok // 2
    group_ids = jnp.arange(groups, dtype=jnp.int32)
    member = expert_ids[:, :, None] == group_ids[None, None, :]
    routed = jnp.any(member, axis=1)
    routed_int = routed.astype(jnp.int32)
    position = jnp.cumsum(routed_int, axis=0) - routed_int
    weight_of = jnp.sum(
        jnp.where(member, gate_weights[:, :, None].astype(jnp.float32), jnp.float32(0.0)), axis=1
    )
    slot_ids = jnp.arange(capacity, dtype=jnp.int32)
    landing = routed[:, :, None] & (position[:, :, None] == slot_ids[None, None, :])
    token_of = jnp.sum(
        jnp.where(landing, jnp.arange(count_tok, dtype=jnp.int32)[:, None, None], 0), axis=0
    )
    filled = jnp.any(landing, axis=0)
    send_weight = jnp.where(
        filled, weight_of[token_of, group_ids[:, None]], jnp.float32(0.0)
    ).astype(jnp.bfloat16)

    def pack_rows(source):
        return jnp.where(filled[:, :, None], source[token_of], jnp.zeros((), source.dtype))

    slice_in, slice_grad, recv_weight = (
        lax.all_to_all(pack_rows(hidden_in), "node", split_axis=0, concat_axis=0, tiled=True),
        lax.all_to_all(pack_rows(out_grad), "node", split_axis=0, concat_axis=0, tiled=True),
        lax.all_to_all(send_weight, "node", split_axis=0, concat_axis=0, tiled=True),
    )
    rows_in, rows_grad = (
        lax.all_gather(slice_in, "expert", axis=2, tiled=True),
        lax.all_gather(slice_grad, "expert", axis=2, tiled=True),
    )
    total_rows = groups * capacity
    features = rows_in.shape[2]
    row_weight = recv_weight.reshape(total_rows).astype(jnp.float32)
    gate_mat = w_gate[0]
    up_mat = w_up[0]
    grad_gate, grad_up, grad_down, grad_gate_pre, grad_up_pre, statistic = expert_backward(
        rows_in.reshape(total_rows, features),
        rows_grad.reshape(total_rows, features),
        row_weight,
        gate_mat,
        up_mat,
        w_down[0],
    )
    input_part = jnp.dot(grad_gate_pre, gate_mat, preferred_element_type=jnp.float32) + jnp.dot(
        grad_up_pre, up_mat, preferred_element_type=jnp.float32
    )
    input_slice = lax.psum_scatter(input_part, "expert", scatter_dimension=1, tiled=True)
    stat_total = lax.psum(statistic, "expert")
    slice_width = input_slice.shape[1]
    back_input, back_stat = (
        lax.all_to_all(
            input_slice.reshape(groups, capacity, slice_width),
            "node",
            split_axis=0,
            concat_axis=0,
            tiled=True,
        ),
        lax.all_to_all(
            stat_total.reshape(groups, capacity), "node", split_axis=0, concat_axis=0, tiled=True
        ),
    )
    flat_input = back_input.reshape(total_rows, slice_width)
    flat_stat = back_stat.reshape(total_rows)
    flat_index = expert_ids * capacity + jnp.take_along_axis(position, expert_ids, axis=1)
    grad_in = (flat_input[flat_index[:, 0]] + flat_input[flat_index[:, 1]]).astype(jnp.bfloat16)
    grad_gates = flat_stat[flat_index]
    return (grad_in, grad_gates, grad_gate[None], grad_up[None], grad_down[None])


def local(hidden_in, *rest):
    if lax.axis_size("expert") == 4 and hidden_in.shape[1] % 128 == 0:
        return fast_local(hidden_in, *rest)
    return general_local(hidden_in, *rest)


def solution(mesh):
    return jax.shard_map(
        local,
        mesh=mesh,
        in_specs=(
            P(("parts", "node"), "expert"),
            P(("parts", "node"), "expert"),
            P(("parts", "node"), None),
            P(("parts", "node"), None),
            P("node", "expert", None),
            P("node", "expert", None),
            P("node", "expert", None),
        ),
        out_specs=(
            P(("parts", "node"), "expert"),
            P(("parts", "node"), None),
            P(("parts", "node"), "expert", None),
            P(("parts", "node"), "expert", None),
            P(("parts", "node"), "expert", None),
        ),
        check_vma=False,
    )
```

```python
import functools

import jax
import jax.numpy as jnp
from jax import lax
from jax.experimental import pallas as pl
from jax.experimental.pallas import tpu as pltpu
from jax.sharding import PartitionSpec as P

BF16 = jnp.bfloat16
F32 = jnp.float32
MIB = 1 << 20


def dot_nt(left, right):
    return lax.dot_general(left, right, (((1,), (1,)), ((), ())), preferred_element_type=F32)


def dot_tn(left, right):
    return lax.dot_general(left, right, (((0,), (0,)), ((), ())), preferred_element_type=F32)


def dot_nn(left, right):
    return lax.dot_general(left, right, (((1,), (0,)), ((), ())), preferred_element_type=F32)


def call(kernel, outs, *args, flops=0, nbytes=0, vmem=6 * MIB, scratch=(), in_hbm=()):
    args = [
        pltpu.with_memory_space_constraint(a, pltpu.HBM) if i in in_hbm else a for i, a in enumerate(args)
    ]
    return pl.pallas_call(
        kernel,
        out_shape=outs,
        in_specs=[
            pl.BlockSpec(memory_space=pltpu.HBM if i in in_hbm else pltpu.VMEM) for i in range(len(args))
        ],
        out_specs=[pl.BlockSpec(memory_space=pltpu.VMEM)] * len(outs),
        scratch_shapes=list(scratch),
        compiler_params=pltpu.CompilerParams(vmem_limit_bytes=vmem),
        cost_estimate=pl.CostEstimate(flops=flops, bytes_accessed=nbytes, transcendentals=0),
    )(*args)


def slots_of(ids, expert, capacity):
    tokens = ids.shape[1]
    routed = jnp.max((ids == expert).astype(F32), axis=0, keepdims=True)
    before = (
        lax.broadcasted_iota(jnp.int32, (tokens, tokens), 0)
        < lax.broadcasted_iota(jnp.int32, (tokens, tokens), 1)
    ).astype(BF16)
    position = dot_nn(jnp.broadcast_to(routed, (8, tokens)).astype(BF16), before)[0:1]
    slot = lax.broadcasted_iota(jnp.int32, (capacity, tokens), 0).astype(F32)
    return jnp.where((slot == position) & (routed > 0.0), 1.0, 0.0)


def pack_kernel(groups, *refs):
    sources, outs, local, sems = refs[:4], refs[4 : 4 + groups], refs[4 + groups : 8 + groups], refs[-1]
    copies = [pltpu.make_async_copy(a, b, sems.at[i]) for i, (a, b) in enumerate(zip(sources, local))]
    for copy in copies:
        copy.start()
    ids_ref, gates_ref, hidden_ref, grad_ref = local
    me = lax.axis_index("node")
    copies[0].wait()
    copies[1].wait()
    ids = ids_ref[...]
    capacity = ids.shape[1] // 2
    one_hots = [slots_of(ids, me ^ shift, capacity) for shift in range(groups)]
    copies[2].wait()
    for one_hot, out in zip(one_hots, outs):
        out[:capacity] = dot_nn(one_hot.astype(BF16), hidden_ref[...]).astype(BF16)
    gates = gates_ref[...].astype(F32)
    copies[3].wait()
    for shift, (one_hot, out) in enumerate(zip(one_hots, outs)):
        weight = jnp.sum(jnp.where(ids == (me ^ shift), gates, 0.0), axis=0, keepdims=True)
        out[capacity:] = dot_nn((one_hot * weight).astype(BF16), grad_ref[...]).astype(BF16)


def pick_kernel(groups, ids_ref, out_ref):
    me = lax.axis_index("node")
    ids = ids_ref[...]
    capacity = ids.shape[1] // 2
    for shift in range(groups):
        chosen = slots_of(ids, me ^ shift, capacity)
        out_ref[:, shift * capacity : (shift + 1) * capacity] = chosen.T.astype(BF16)


def load_kernel(*refs):
    count = len(refs) // 2
    sources, outs, sems = refs[:count], refs[count : 2 * count], refs[-1]
    copies = [pltpu.make_async_copy(a, b, sems.at[i]) for i, (a, b) in enumerate(zip(sources, outs))]
    for copy in copies:
        copy.start()
    for copy in copies:
        copy.wait()


def assemble(parts, relatives, groups, base, rows_ref, grads_ref):
    me = lax.axis_index("expert")
    capacity, width = parts[0].shape[0] // 2, parts[0].shape[1]
    for index, part in enumerate(parts):
        place, shift = divmod(index, groups)
        columns = pl.ds(pl.multiple_of(((me ^ relatives[place]) - base) * width, width), width)
        rows = slice(shift * capacity, (shift + 1) * capacity)
        rows_ref[rows, columns] = part[:capacity]
        grads_ref[rows, columns] = part[capacity:]


def local_kernel(groups, *refs):
    parts = refs[: 2 * groups]
    gate_w, up_w, down_w, gate_ref, up_ref, back_ref, rows_ref, grads_ref = refs[2 * groups :]
    base = (lax.axis_index("expert") // 2) * 2
    assemble(parts, (0, 1), groups, base, rows_ref, grads_ref)
    half = rows_ref.shape[1]
    columns = pl.ds(pl.multiple_of(base * (half // 2), half), half)
    gate_ref[...] = dot_nt(gate_w[0, :, columns], rows_ref[...])
    up_ref[...] = dot_nt(up_w[0, :, columns], rows_ref[...])
    back_ref[...] = dot_nt(down_w[0, :, columns], grads_ref[...])


def middle_kernel(groups, *refs):
    parts = refs[: 4 * groups]
    (gate_w, up_w, down_w, gate_ref, up_ref, back_ref,
     rows_ref, grads_ref, dgate_ref, dup_ref, hid_ref, stat_ref) = refs[4 * groups :]
    assemble(parts, (2, 3, 0, 1), groups, 0, rows_ref, grads_ref)
    half = rows_ref.shape[1] // 2
    columns = pl.ds(pl.multiple_of((1 - lax.axis_index("expert") // 2) * half, half), half)
    gate = gate_ref[...] + dot_nt(gate_w[0, :, columns], rows_ref[:, columns])
    up = up_ref[...] + dot_nt(up_w[0, :, columns], rows_ref[:, columns])
    back = back_ref[...] + dot_nt(down_w[0, :, columns], grads_ref[:, columns])
    sig = 1.0 / (1.0 + jnp.exp(-gate))
    silu = gate * sig
    hidden = silu * up
    stat_ref[...] = jnp.broadcast_to(jnp.sum(hidden * back, axis=0, keepdims=True), stat_ref.shape)
    dgate_ref[...] = (back * up * sig * (1.0 + gate * (1.0 - sig))).astype(BF16)
    dup_ref[...] = (back * silu).astype(BF16)
    hid_ref[...] = hidden.astype(BF16)


EXTRA = 8


def halves_of(row):
    high = row.astype(BF16).astype(F32)
    index = lax.broadcasted_iota(jnp.int32, (EXTRA, row.shape[1]), 0)
    return jnp.where(index == 0, high, jnp.where(index == 1, row - high, 0.0)).astype(BF16)


def row_of(halves):
    return halves[0:1].astype(F32) + halves[1:2].astype(F32)


def input_kernel(relative, dgate_ref, dup_ref, gate_w, up_w, stat_ref, out_ref):
    me = lax.axis_index("expert")
    rows, width = dgate_ref.shape[1], out_ref.shape[1]
    columns = pl.ds(pl.multiple_of((me ^ relative) * width, width), width)
    total = dot_tn(dgate_ref[...], gate_w[0, :, columns]) + dot_tn(dup_ref[...], up_w[0, :, columns])
    out_ref[:rows] = total.astype(out_ref.dtype)
    if out_ref.shape[0] > rows:
        out_ref[rows:, :rows] = halves_of(stat_ref[0:1])
        out_ref[rows:, rows:] = jnp.zeros((EXTRA, width - rows), BF16)


def add_kernel(groups, keep, got, stat_ref, *outs):
    capacity = outs[0].shape[0] - EXTRA
    rows = groups * capacity
    stat = stat_ref[0:1] + row_of(got[rows:, :rows])
    outs[groups][...] = jnp.broadcast_to(stat, outs[groups].shape)
    for shift in range(groups):
        block = slice(shift * capacity, (shift + 1) * capacity)
        outs[shift][:capacity] = (keep[block] + got[block].astype(F32)).astype(BF16)
        outs[shift][capacity:, :capacity] = halves_of(stat[:, block])
        outs[shift][capacity:, capacity:] = jnp.zeros((EXTRA, outs[shift].shape[1] - capacity), BF16)


def join_kernel(shift, keep, got, crossed, stat_ref, out):
    capacity = out.shape[0] - EXTRA
    block = slice(shift * capacity, (shift + 1) * capacity)
    out[:capacity] = (keep[block] + got[block].astype(F32) + crossed[:capacity].astype(F32)).astype(BF16)
    out[capacity:, :capacity] = halves_of(stat_ref[0:1, block] + row_of(crossed[capacity:, :capacity]))
    out[capacity:, capacity:] = jnp.zeros((EXTRA, out.shape[1] - capacity), BF16)


def grad_kernel(tile, left_ref, rows_ref, out_ref, held_ref, sems):
    copies = []
    for index in range(rows_ref.shape[1] // tile):
        columns = slice(index * tile, (index + 1) * tile)
        held_ref[:, columns] = dot_nn(left_ref[...], rows_ref[:, columns]).astype(BF16)
        copies.append(pltpu.make_async_copy(held_ref.at[:, columns], out_ref.at[0, :, columns], sems.at[index]))
        copies[-1].start()
    for copy in copies:
        copy.wait()


def weight_grad(left, rows):
    units, features = left.shape[0], rows.shape[1]
    tile = 512 if features % 512 == 0 else features
    return pl.pallas_call(
        functools.partial(grad_kernel, tile),
        out_shape=jax.ShapeDtypeStruct((1, units, features), BF16),
        in_specs=[pl.BlockSpec(memory_space=pltpu.VMEM)] * 2,
        out_specs=pl.BlockSpec(memory_space=pltpu.HBM),
        scratch_shapes=[pltpu.VMEM((units, features), BF16), pltpu.SemaphoreType.DMA((features // tile,))],
        compiler_params=pltpu.CompilerParams(vmem_limit_bytes=10 * MIB),
        cost_estimate=pl.CostEstimate(flops=0, bytes_accessed=0, transcendentals=0),
    )(left, rows)


def finish_kernel(groups, ids_ref, gates_in_ref, pick_ref, *refs):
    parts = refs[:groups]
    grad_ref, gates_ref, rows_ref = refs[groups:]
    me = lax.axis_index("node")
    ids = ids_ref[...]
    capacity = ids.shape[1] // 2
    for shift in range(groups):
        rows_ref[shift * capacity : (shift + 1) * capacity] = parts[shift][:capacity]
    grad_ref[...] = dot_nn(pick_ref[...], rows_ref[...]).astype(BF16)
    gates = jnp.zeros(ids.shape, F32)
    for shift in range(groups):
        columns = slice(shift * capacity, (shift + 1) * capacity)
        halves = dot_nt(parts[shift][capacity:, :capacity], pick_ref[:, columns])
        gates = gates + jnp.where(ids == (me ^ shift), halves[0:1] + halves[1:2], 0.0)
    gates_ref[...] = gates / gates_in_ref[...].astype(F32)


def fast_local(hidden_in, out_grad, expert_ids, gate_weights, w_gate, w_up, w_down):
    groups = lax.axis_size("node")
    experts = lax.axis_size("expert")
    tokens, width = hidden_in.shape
    capacity = tokens // 2
    rows = groups * capacity
    units, features = w_gate.shape[1:]
    shape = jax.ShapeDtypeStruct
    after = lax.optimization_barrier

    def over_node(x, shift):
        return lax.ppermute(x, "node", [(i, i ^ shift) for i in range(groups)])

    def over_expert(x, relative):
        return lax.ppermute(x, "expert", [(i, i ^ relative) for i in range(experts)])

    ids, gates = expert_ids.T, gate_weights.T
    blocks = call(
        functools.partial(pack_kernel, groups),
        [shape((tokens, width), BF16)] * groups,
        ids, gates, hidden_in, out_grad,
        flops=4 * rows * tokens * width, nbytes=6 * tokens * width, in_hbm=(0, 1, 2, 3),
        scratch=[
            pltpu.VMEM(ids.shape, ids.dtype), pltpu.VMEM(gates.shape, gates.dtype),
            pltpu.VMEM((tokens, width), BF16), pltpu.VMEM((tokens, width), BF16), pltpu.SemaphoreType.DMA((4,)),
        ],
    )
    own = list(blocks)
    partner, other = [None] * groups, [None] * groups
    other[0] = over_expert(own[0], 2)
    partner[0] = over_expert(own[0], 1)
    own[1] = over_node(blocks[1], 1)
    partner[1] = over_expert(own[1], 1)
    own[2] = over_node(blocks[2], 2)
    partner[2] = over_expert(own[2], 1)
    own[3] = over_node(blocks[3], 3)
    partner[3] = over_expert(own[3], 1)
    mats = after((w_gate, w_up, w_down, other[0]))[:3]
    mats = call(load_kernel, [shape(m.shape, BF16) for m in mats], *mats, nbytes=12 * units * features,
                in_hbm=(0, 1, 2), scratch=[pltpu.SemaphoreType.DMA((3,))])
    other[1] = over_expert(own[1], 2)
    other[2] = over_expert(own[2], 2)
    other[3] = over_expert(after((own[3], other[0], other[2]))[0], 2)
    across = [over_expert(x, 1) for x in other[:-1]]

    dense = 2 * rows * units * features
    partial_sums = call(
        functools.partial(local_kernel, groups),
        [shape((units, rows), F32)] * 3,
        *own, *partner, *mats, flops=3 * dense // 2, nbytes=3 * units * features,
        scratch=[pltpu.VMEM((rows, 2 * width), BF16)] * 2,
    )
    across.append(over_expert(after((other[-1], partial_sums[0]))[0], 1))
    rows_in, rows_grad, dgate, dup, hid, stat = call(
        functools.partial(middle_kernel, groups),
        [shape((rows, features), BF16)] * 2 + [shape((units, rows), BF16)] * 3 + [shape((8, rows), F32)],
        *other, *across, *own, *partner, *mats, *partial_sums,
        flops=3 * dense // 2, nbytes=3 * units * features,
    )

    def input_part(relative, extra, kind):
        return call(
            functools.partial(input_kernel, relative), [shape((rows + extra, width), kind)],
            dgate, dup, mats[0], mats[1], stat, flops=dense // 2, nbytes=units * features,
        )[0]

    far_got = over_expert(input_part(3, EXTRA, BF16), 1)
    near_got = over_expert(input_part(1, 0, BF16), 1)
    far_keep = input_part(2, 0, F32)
    *far_sum, stat_pair = call(
        functools.partial(add_kernel, groups),
        [shape((capacity + EXTRA, width), BF16)] * groups + [shape((8, rows), F32)],
        far_keep, far_got, stat, nbytes=6 * rows * width,
    )
    near_keep = input_part(0, 0, F32)
    back, totals = [None] * groups, []
    for s in reversed(range(groups)):
        totals += call(functools.partial(join_kernel, s), [shape((capacity + EXTRA, width), BF16)],
                       near_keep, near_got, over_expert(far_sum[s], 2), stat_pair)
        back[s] = over_node(totals[-1], s) if s else totals[-1]

    dgate, dup, hid, _ = after((dgate, dup, hid, tuple(totals[:-1])))
    weight_grads = [weight_grad(dgate, rows_in), weight_grad(dup, rows_in), weight_grad(hid, rows_grad)]

    pick = call(functools.partial(pick_kernel, groups), [shape((tokens, rows), BF16)], after((ids, own[1]))[0])[0]
    grad_in, grad_gates = call(
        functools.partial(finish_kernel, groups),
        [shape((tokens, width), BF16), shape(ids.shape, F32)],
        ids, gates, pick, *back, scratch=[pltpu.VMEM((rows, width), BF16)],
    )
    return (grad_in, grad_gates.T, *weight_grads)


def contract_rows(left, right):
    return lax.dot_general(
        left, right, (((0,), (0,)), ((), ())), preferred_element_type=jnp.float32
    )


def contract_cols(left, right):
    return lax.dot_general(
        left, right, (((1,), (1,)), ((), ())), preferred_element_type=jnp.float32
    )


def expert_backward(rows_in, rows_grad, row_weight, gate_mat, up_mat, down_mat):
    gate_pre = contract_cols(rows_in, gate_mat)
    up_pre = contract_cols(rows_in, up_mat)
    sigmoid_gate = jax.nn.sigmoid(gate_pre)
    silu_gate = gate_pre * sigmoid_gate
    hidden = silu_gate * up_pre
    back_hidden = contract_cols(rows_grad, down_mat)
    statistic = jnp.sum(hidden * back_hidden, axis=1)
    scaled = row_weight[:, None] * back_hidden
    grad_gate_pre = (
        scaled * up_pre * sigmoid_gate * (1.0 + gate_pre * (1.0 - sigmoid_gate))
    ).astype(jnp.bfloat16)
    grad_up_pre = (scaled * silu_gate).astype(jnp.bfloat16)
    weighted_hidden = (row_weight[:, None] * hidden).astype(jnp.bfloat16)
    grad_down = contract_rows(weighted_hidden, rows_grad).astype(jnp.bfloat16)
    grad_gate = contract_rows(grad_gate_pre, rows_in).astype(jnp.bfloat16)
    grad_up = contract_rows(grad_up_pre, rows_in).astype(jnp.bfloat16)
    return (grad_gate, grad_up, grad_down, grad_gate_pre, grad_up_pre, statistic)


def general_local(hidden_in, out_grad, expert_ids, gate_weights, w_gate, w_up, w_down):
    groups = lax.axis_size("node")
    count_tok = hidden_in.shape[0]
    capacity = count_tok // 2
    group_ids = jnp.arange(groups, dtype=jnp.int32)
    member = expert_ids[:, :, None] == group_ids[None, None, :]
    routed = jnp.any(member, axis=1)
    routed_int = routed.astype(jnp.int32)
    position = jnp.cumsum(routed_int, axis=0) - routed_int
    weight_of = jnp.sum(
        jnp.where(member, gate_weights[:, :, None].astype(jnp.float32), jnp.float32(0.0)), axis=1
    )
    slot_ids = jnp.arange(capacity, dtype=jnp.int32)
    landing = routed[:, :, None] & (position[:, :, None] == slot_ids[None, None, :])
    token_of = jnp.sum(
        jnp.where(landing, jnp.arange(count_tok, dtype=jnp.int32)[:, None, None], 0), axis=0
    )
    filled = jnp.any(landing, axis=0)
    send_weight = jnp.where(
        filled, weight_of[token_of, group_ids[:, None]], jnp.float32(0.0)
    ).astype(jnp.bfloat16)

    def pack_rows(source):
        return jnp.where(filled[:, :, None], source[token_of], jnp.zeros((), source.dtype))

    slice_in, slice_grad, recv_weight = (
        lax.all_to_all(pack_rows(hidden_in), "node", split_axis=0, concat_axis=0, tiled=True),
        lax.all_to_all(pack_rows(out_grad), "node", split_axis=0, concat_axis=0, tiled=True),
        lax.all_to_all(send_weight, "node", split_axis=0, concat_axis=0, tiled=True),
    )
    rows_in, rows_grad = (
        lax.all_gather(slice_in, "expert", axis=2, tiled=True),
        lax.all_gather(slice_grad, "expert", axis=2, tiled=True),
    )
    total_rows = groups * capacity
    features = rows_in.shape[2]
    row_weight = recv_weight.reshape(total_rows).astype(jnp.float32)
    gate_mat = w_gate[0]
    up_mat = w_up[0]
    grad_gate, grad_up, grad_down, grad_gate_pre, grad_up_pre, statistic = expert_backward(
        rows_in.reshape(total_rows, features),
        rows_grad.reshape(total_rows, features),
        row_weight,
        gate_mat,
        up_mat,
        w_down[0],
    )
    input_part = jnp.dot(grad_gate_pre, gate_mat, preferred_element_type=jnp.float32) + jnp.dot(
        grad_up_pre, up_mat, preferred_element_type=jnp.float32
    )
    input_slice = lax.psum_scatter(input_part, "expert", scatter_dimension=1, tiled=True)
    stat_total = lax.psum(statistic, "expert")
    slice_width = input_slice.shape[1]
    back_input, back_stat = (
        lax.all_to_all(
            input_slice.reshape(groups, capacity, slice_width),
            "node",
            split_axis=0,
            concat_axis=0,
            tiled=True,
        ),
        lax.all_to_all(
            stat_total.reshape(groups, capacity), "node", split_axis=0, concat_axis=0, tiled=True
        ),
    )
    flat_input = back_input.reshape(total_rows, slice_width)
    flat_stat = back_stat.reshape(total_rows)
    flat_index = expert_ids * capacity + jnp.take_along_axis(position, expert_ids, axis=1)
    grad_in = (flat_input[flat_index[:, 0]] + flat_input[flat_index[:, 1]]).astype(jnp.bfloat16)
    grad_gates = flat_stat[flat_index]
    return (grad_in, grad_gates, grad_gate[None], grad_up[None], grad_down[None])


def local(hidden_in, *rest):
    if lax.axis_size("expert") == 4 and hidden_in.shape[1] % 128 == 0:
        return fast_local(hidden_in, *rest)
    return general_local(hidden_in, *rest)


def solution(mesh):
    return jax.shard_map(
        local,
        mesh=mesh,
        in_specs=(
            P(("parts", "node"), "expert"),
            P(("parts", "node"), "expert"),
            P(("parts", "node"), None),
            P(("parts", "node"), None),
            P("node", "expert", None),
            P("node", "expert", None),
            P("node", "expert", None),
        ),
        out_specs=(
            P(("parts", "node"), "expert"),
            P(("parts", "node"), None),
            P(("parts", "node"), "expert", None),
            P(("parts", "node"), "expert", None),
            P(("parts", "node"), "expert", None),
        ),
        check_vma=False,
    )
```

```python
import functools

import jax
import jax.numpy as jnp
from jax import lax
from jax.experimental import pallas as pl
from jax.experimental.pallas import tpu as pltpu
from jax.sharding import PartitionSpec as P

BF16 = jnp.bfloat16
F32 = jnp.float32
MIB = 1 << 20


def dot_nt(left, right):
    return lax.dot_general(left, right, (((1,), (1,)), ((), ())), preferred_element_type=F32)


def dot_tn(left, right):
    return lax.dot_general(left, right, (((0,), (0,)), ((), ())), preferred_element_type=F32)


def dot_nn(left, right):
    return lax.dot_general(left, right, (((1,), (0,)), ((), ())), preferred_element_type=F32)


def call(kernel, outs, *args, flops=0, nbytes=0, vmem=6 * MIB, scratch=(), in_hbm=()):
    args = [
        pltpu.with_memory_space_constraint(a, pltpu.HBM) if i in in_hbm else a for i, a in enumerate(args)
    ]
    return pl.pallas_call(
        kernel,
        out_shape=outs,
        in_specs=[
            pl.BlockSpec(memory_space=pltpu.HBM if i in in_hbm else pltpu.VMEM) for i in range(len(args))
        ],
        out_specs=[pl.BlockSpec(memory_space=pltpu.VMEM)] * len(outs),
        scratch_shapes=list(scratch),
        compiler_params=pltpu.CompilerParams(vmem_limit_bytes=vmem),
        cost_estimate=pl.CostEstimate(flops=flops, bytes_accessed=nbytes, transcendentals=0),
    )(*args)


def slots_of(ids, expert, capacity):
    tokens = ids.shape[1]
    routed = jnp.max((ids == expert).astype(F32), axis=0, keepdims=True)
    before = (
        lax.broadcasted_iota(jnp.int32, (tokens, tokens), 0)
        < lax.broadcasted_iota(jnp.int32, (tokens, tokens), 1)
    ).astype(BF16)
    position = dot_nn(jnp.broadcast_to(routed, (8, tokens)).astype(BF16), before)[0:1]
    slot = lax.broadcasted_iota(jnp.int32, (capacity, tokens), 0).astype(F32)
    return jnp.where((slot == position) & (routed > 0.0), 1.0, 0.0)


def pack_kernel(groups, *refs):
    sources, outs, local, sems = refs[:4], refs[4 : 4 + groups], refs[4 + groups : 8 + groups], refs[-1]
    copies = [pltpu.make_async_copy(a, b, sems.at[i]) for i, (a, b) in enumerate(zip(sources, local))]
    for copy in copies:
        copy.start()
    ids_ref, gates_ref, hidden_ref, grad_ref = local
    me = lax.axis_index("node")
    copies[0].wait()
    copies[1].wait()
    ids = ids_ref[...]
    capacity = ids.shape[1] // 2
    one_hots = [slots_of(ids, me ^ shift, capacity) for shift in range(groups)]
    copies[2].wait()
    for one_hot, out in zip(one_hots, outs):
        out[:capacity] = dot_nn(one_hot.astype(BF16), hidden_ref[...]).astype(BF16)
    gates = gates_ref[...].astype(F32)
    copies[3].wait()
    for shift, (one_hot, out) in enumerate(zip(one_hots, outs)):
        weight = jnp.sum(jnp.where(ids == (me ^ shift), gates, 0.0), axis=0, keepdims=True)
        out[capacity:] = dot_nn((one_hot * weight).astype(BF16), grad_ref[...]).astype(BF16)


def pick_kernel(groups, ids_ref, out_ref):
    me = lax.axis_index("node")
    ids = ids_ref[...]
    capacity = ids.shape[1] // 2
    for shift in range(groups):
        chosen = slots_of(ids, me ^ shift, capacity)
        out_ref[:, shift * capacity : (shift + 1) * capacity] = chosen.T.astype(BF16)


def load_kernel(*refs):
    count = len(refs) // 2
    sources, outs, sems = refs[:count], refs[count : 2 * count], refs[-1]
    copies = [pltpu.make_async_copy(a, b, sems.at[i]) for i, (a, b) in enumerate(zip(sources, outs))]
    for copy in copies:
        copy.start()
    for copy in copies:
        copy.wait()


def assemble(parts, relatives, groups, base, rows_ref, grads_ref):
    me = lax.axis_index("expert")
    capacity, width = parts[0].shape[0] // 2, parts[0].shape[1]
    for index, part in enumerate(parts):
        place, shift = divmod(index, groups)
        columns = pl.ds(pl.multiple_of(((me ^ relatives[place]) - base) * width, width), width)
        rows = slice(shift * capacity, (shift + 1) * capacity)
        rows_ref[rows, columns] = part[:capacity]
        grads_ref[rows, columns] = part[capacity:]


def local_kernel(groups, *refs):
    parts = refs[: 2 * groups]
    gate_w, up_w, down_w, gate_ref, up_ref, back_ref, rows_ref, grads_ref = refs[2 * groups :]
    base = (lax.axis_index("expert") // 2) * 2
    assemble(parts, (0, 1), groups, base, rows_ref, grads_ref)
    half = rows_ref.shape[1]
    columns = pl.ds(pl.multiple_of(base * (half // 2), half), half)
    gate_ref[...] = dot_nt(gate_w[0, :, columns], rows_ref[...])
    up_ref[...] = dot_nt(up_w[0, :, columns], rows_ref[...])
    back_ref[...] = dot_nt(down_w[0, :, columns], grads_ref[...])


def middle_kernel(groups, *refs):
    parts = refs[: 4 * groups]
    (gate_w, up_w, down_w, gate_ref, up_ref, back_ref,
     rows_ref, grads_ref, dgate_ref, dup_ref, hid_ref, stat_ref) = refs[4 * groups :]
    assemble(parts, (2, 3, 0, 1), groups, 0, rows_ref, grads_ref)
    half = rows_ref.shape[1] // 2
    columns = pl.ds(pl.multiple_of((1 - lax.axis_index("expert") // 2) * half, half), half)
    gate = gate_ref[...] + dot_nt(gate_w[0, :, columns], rows_ref[:, columns])
    up = up_ref[...] + dot_nt(up_w[0, :, columns], rows_ref[:, columns])
    back = back_ref[...] + dot_nt(down_w[0, :, columns], grads_ref[:, columns])
    sig = 1.0 / (1.0 + jnp.exp(-gate))
    silu = gate * sig
    hidden = silu * up
    stat_ref[...] = jnp.broadcast_to(jnp.sum(hidden * back, axis=0, keepdims=True), stat_ref.shape)
    dgate_ref[...] = (back * up * sig * (1.0 + gate * (1.0 - sig))).astype(BF16)
    dup_ref[...] = (back * silu).astype(BF16)
    hid_ref[...] = hidden.astype(BF16)


EXTRA = 8


def halves_of(row):
    high = row.astype(BF16).astype(F32)
    index = lax.broadcasted_iota(jnp.int32, (EXTRA, row.shape[1]), 0)
    return jnp.where(index == 0, high, jnp.where(index == 1, row - high, 0.0)).astype(BF16)


def row_of(halves):
    return halves[0:1].astype(F32) + halves[1:2].astype(F32)


def input_kernel(relative, dgate_ref, dup_ref, gate_w, up_w, stat_ref, out_ref):
    me = lax.axis_index("expert")
    rows, width = dgate_ref.shape[1], out_ref.shape[1]
    columns = pl.ds(pl.multiple_of((me ^ relative) * width, width), width)
    total = dot_tn(dgate_ref[...], gate_w[0, :, columns]) + dot_tn(dup_ref[...], up_w[0, :, columns])
    out_ref[:rows] = total.astype(out_ref.dtype)
    if out_ref.shape[0] > rows:
        out_ref[rows:, :rows] = halves_of(stat_ref[0:1])
        out_ref[rows:, rows:] = jnp.zeros((EXTRA, width - rows), BF16)


def add_kernel(groups, keep, got, stat_ref, *outs):
    capacity = outs[0].shape[0] - EXTRA
    rows = groups * capacity
    stat = stat_ref[0:1] + row_of(got[rows:, :rows])
    outs[groups][...] = jnp.broadcast_to(stat, outs[groups].shape)
    for shift in range(groups):
        block = slice(shift * capacity, (shift + 1) * capacity)
        outs[shift][:capacity] = (keep[block] + got[block].astype(F32)).astype(BF16)
        outs[shift][capacity:, :capacity] = halves_of(stat[:, block])
        outs[shift][capacity:, capacity:] = jnp.zeros((EXTRA, outs[shift].shape[1] - capacity), BF16)


def join_kernel(shift, keep, got, crossed, stat_ref, out):
    capacity = out.shape[0] - EXTRA
    block = slice(shift * capacity, (shift + 1) * capacity)
    out[:capacity] = (keep[block] + got[block].astype(F32) + crossed[:capacity].astype(F32)).astype(BF16)
    out[capacity:, :capacity] = halves_of(stat_ref[0:1, block] + row_of(crossed[capacity:, :capacity]))
    out[capacity:, capacity:] = jnp.zeros((EXTRA, out.shape[1] - capacity), BF16)


def grad_kernel(tile, left_ref, rows_ref, out_ref, held_ref, sems):
    copies = []
    for index in range(rows_ref.shape[1] // tile):
        columns = slice(index * tile, (index + 1) * tile)
        held_ref[:, columns] = dot_nn(left_ref[...], rows_ref[:, columns]).astype(BF16)
        copies.append(pltpu.make_async_copy(held_ref.at[:, columns], out_ref.at[0, :, columns], sems.at[index]))
        copies[-1].start()
    for copy in copies:
        copy.wait()


def weight_grad(left, rows):
    units, features = left.shape[0], rows.shape[1]
    tile = 512 if features % 512 == 0 else features
    return pl.pallas_call(
        functools.partial(grad_kernel, tile),
        out_shape=jax.ShapeDtypeStruct((1, units, features), BF16),
        in_specs=[pl.BlockSpec(memory_space=pltpu.VMEM)] * 2,
        out_specs=pl.BlockSpec(memory_space=pltpu.HBM),
        scratch_shapes=[pltpu.VMEM((units, features), BF16), pltpu.SemaphoreType.DMA((features // tile,))],
        compiler_params=pltpu.CompilerParams(vmem_limit_bytes=10 * MIB),
        cost_estimate=pl.CostEstimate(flops=0, bytes_accessed=0, transcendentals=0),
    )(left, rows)


def finish_kernel(groups, ids_ref, gates_in_ref, pick_ref, *refs):
    parts = refs[:groups]
    grad_ref, gates_ref, rows_ref = refs[groups:]
    me = lax.axis_index("node")
    ids = ids_ref[...]
    capacity = ids.shape[1] // 2
    for shift in range(groups):
        rows_ref[shift * capacity : (shift + 1) * capacity] = parts[shift][:capacity]
    grad_ref[...] = dot_nn(pick_ref[...], rows_ref[...]).astype(BF16)
    gates = jnp.zeros(ids.shape, F32)
    for shift in range(groups):
        columns = slice(shift * capacity, (shift + 1) * capacity)
        halves = dot_nt(parts[shift][capacity:, :capacity], pick_ref[:, columns])
        gates = gates + jnp.where(ids == (me ^ shift), halves[0:1] + halves[1:2], 0.0)
    gates_ref[...] = gates / gates_in_ref[...].astype(F32)


def fast_local(hidden_in, out_grad, expert_ids, gate_weights, w_gate, w_up, w_down):
    groups = lax.axis_size("node")
    experts = lax.axis_size("expert")
    tokens, width = hidden_in.shape
    capacity = tokens // 2
    rows = groups * capacity
    units, features = w_gate.shape[1:]
    shape = jax.ShapeDtypeStruct
    after = lax.optimization_barrier

    def over_node(x, shift):
        return lax.ppermute(x, "node", [(i, i ^ shift) for i in range(groups)])

    def over_expert(x, relative):
        return lax.ppermute(x, "expert", [(i, i ^ relative) for i in range(experts)])

    ids, gates = expert_ids.T, gate_weights.T
    blocks = call(
        functools.partial(pack_kernel, groups),
        [shape((tokens, width), BF16)] * groups,
        ids, gates, hidden_in, out_grad,
        flops=4 * rows * tokens * width, nbytes=6 * tokens * width, in_hbm=(0, 1, 2, 3),
        scratch=[
            pltpu.VMEM(ids.shape, ids.dtype), pltpu.VMEM(gates.shape, gates.dtype),
            pltpu.VMEM((tokens, width), BF16), pltpu.VMEM((tokens, width), BF16), pltpu.SemaphoreType.DMA((4,)),
        ],
    )
    own = list(blocks)
    partner, other = [None] * groups, [None] * groups
    other[0] = over_expert(own[0], 2)
    partner[0] = over_expert(own[0], 1)
    own[3] = over_node(blocks[3], 3)
    partner[3] = over_expert(own[3], 1)
    own[2] = over_node(blocks[2], 2)
    partner[2] = over_expert(own[2], 1)
    own[1] = over_node(blocks[1], 1)
    partner[1] = over_expert(own[1], 1)
    mats = after((w_gate, w_up, w_down, partner[0]))[:3]
    mats = call(load_kernel, [shape(m.shape, BF16) for m in mats], *mats, nbytes=12 * units * features,
                in_hbm=(0, 1, 2), scratch=[pltpu.SemaphoreType.DMA((3,))])
    other[1] = over_expert(after((own[1], other[0], mats[0]))[0], 2)
    other[2] = over_expert(after((own[2], mats[0]))[0], 2)
    other[3] = over_expert(after((own[3], other[2]))[0], 2)
    across = [over_expert(x, 1) for x in other[:-1]]

    dense = 2 * rows * units * features
    partial_sums = call(
        functools.partial(local_kernel, groups),
        [shape((units, rows), F32)] * 3,
        *own, *partner, *mats, flops=3 * dense // 2, nbytes=3 * units * features,
        scratch=[pltpu.VMEM((rows, 2 * width), BF16)] * 2,
    )
    across.append(over_expert(after((other[-1], partial_sums[0]))[0], 1))
    rows_in, rows_grad, dgate, dup, hid, stat = call(
        functools.partial(middle_kernel, groups),
        [shape((rows, features), BF16)] * 2 + [shape((units, rows), BF16)] * 3 + [shape((8, rows), F32)],
        *other, *across, *own, *partner, *mats, *partial_sums,
        flops=3 * dense // 2, nbytes=3 * units * features,
    )

    def input_part(relative, extra, kind):
        return call(
            functools.partial(input_kernel, relative), [shape((rows + extra, width), kind)],
            dgate, dup, mats[0], mats[1], stat, flops=dense // 2, nbytes=units * features,
        )[0]

    far_got = over_expert(input_part(3, EXTRA, BF16), 1)
    near_got = over_expert(input_part(1, 0, BF16), 1)
    far_keep = input_part(2, 0, F32)
    *far_sum, stat_pair = call(
        functools.partial(add_kernel, groups),
        [shape((capacity + EXTRA, width), BF16)] * groups + [shape((8, rows), F32)],
        far_keep, far_got, stat, nbytes=6 * rows * width,
    )
    near_keep = input_part(0, 0, F32)
    back, totals = [None] * groups, []
    for s in reversed(range(groups)):
        totals += call(functools.partial(join_kernel, s), [shape((capacity + EXTRA, width), BF16)],
                       near_keep, near_got, over_expert(far_sum[s], 2), stat_pair)
        back[s] = over_node(totals[-1], s) if s else totals[-1]

    dgate, dup, hid, _ = after((dgate, dup, hid, tuple(totals[:-1])))
    weight_grads = [weight_grad(dgate, rows_in), weight_grad(dup, rows_in), weight_grad(hid, rows_grad)]

    pick = call(functools.partial(pick_kernel, groups), [shape((tokens, rows), BF16)], after((ids, own[1]))[0])[0]
    grad_in, grad_gates = call(
        functools.partial(finish_kernel, groups),
        [shape((tokens, width), BF16), shape(ids.shape, F32)],
        ids, gates, pick, *back, scratch=[pltpu.VMEM((rows, width), BF16)],
    )
    return (grad_in, grad_gates.T, *weight_grads)


def contract_rows(left, right):
    return lax.dot_general(
        left, right, (((0,), (0,)), ((), ())), preferred_element_type=jnp.float32
    )


def contract_cols(left, right):
    return lax.dot_general(
        left, right, (((1,), (1,)), ((), ())), preferred_element_type=jnp.float32
    )


def expert_backward(rows_in, rows_grad, row_weight, gate_mat, up_mat, down_mat):
    gate_pre = contract_cols(rows_in, gate_mat)
    up_pre = contract_cols(rows_in, up_mat)
    sigmoid_gate = jax.nn.sigmoid(gate_pre)
    silu_gate = gate_pre * sigmoid_gate
    hidden = silu_gate * up_pre
    back_hidden = contract_cols(rows_grad, down_mat)
    statistic = jnp.sum(hidden * back_hidden, axis=1)
    scaled = row_weight[:, None] * back_hidden
    grad_gate_pre = (
        scaled * up_pre * sigmoid_gate * (1.0 + gate_pre * (1.0 - sigmoid_gate))
    ).astype(jnp.bfloat16)
    grad_up_pre = (scaled * silu_gate).astype(jnp.bfloat16)
    weighted_hidden = (row_weight[:, None] * hidden).astype(jnp.bfloat16)
    grad_down = contract_rows(weighted_hidden, rows_grad).astype(jnp.bfloat16)
    grad_gate = contract_rows(grad_gate_pre, rows_in).astype(jnp.bfloat16)
    grad_up = contract_rows(grad_up_pre, rows_in).astype(jnp.bfloat16)
    return (grad_gate, grad_up, grad_down, grad_gate_pre, grad_up_pre, statistic)


def general_local(hidden_in, out_grad, expert_ids, gate_weights, w_gate, w_up, w_down):
    groups = lax.axis_size("node")
    count_tok = hidden_in.shape[0]
    capacity = count_tok // 2
    group_ids = jnp.arange(groups, dtype=jnp.int32)
    member = expert_ids[:, :, None] == group_ids[None, None, :]
    routed = jnp.any(member, axis=1)
    routed_int = routed.astype(jnp.int32)
    position = jnp.cumsum(routed_int, axis=0) - routed_int
    weight_of = jnp.sum(
        jnp.where(member, gate_weights[:, :, None].astype(jnp.float32), jnp.float32(0.0)), axis=1
    )
    slot_ids = jnp.arange(capacity, dtype=jnp.int32)
    landing = routed[:, :, None] & (position[:, :, None] == slot_ids[None, None, :])
    token_of = jnp.sum(
        jnp.where(landing, jnp.arange(count_tok, dtype=jnp.int32)[:, None, None], 0), axis=0
    )
    filled = jnp.any(landing, axis=0)
    send_weight = jnp.where(
        filled, weight_of[token_of, group_ids[:, None]], jnp.float32(0.0)
    ).astype(jnp.bfloat16)

    def pack_rows(source):
        return jnp.where(filled[:, :, None], source[token_of], jnp.zeros((), source.dtype))

    slice_in, slice_grad, recv_weight = (
        lax.all_to_all(pack_rows(hidden_in), "node", split_axis=0, concat_axis=0, tiled=True),
        lax.all_to_all(pack_rows(out_grad), "node", split_axis=0, concat_axis=0, tiled=True),
        lax.all_to_all(send_weight, "node", split_axis=0, concat_axis=0, tiled=True),
    )
    rows_in, rows_grad = (
        lax.all_gather(slice_in, "expert", axis=2, tiled=True),
        lax.all_gather(slice_grad, "expert", axis=2, tiled=True),
    )
    total_rows = groups * capacity
    features = rows_in.shape[2]
    row_weight = recv_weight.reshape(total_rows).astype(jnp.float32)
    gate_mat = w_gate[0]
    up_mat = w_up[0]
    grad_gate, grad_up, grad_down, grad_gate_pre, grad_up_pre, statistic = expert_backward(
        rows_in.reshape(total_rows, features),
        rows_grad.reshape(total_rows, features),
        row_weight,
        gate_mat,
        up_mat,
        w_down[0],
    )
    input_part = jnp.dot(grad_gate_pre, gate_mat, preferred_element_type=jnp.float32) + jnp.dot(
        grad_up_pre, up_mat, preferred_element_type=jnp.float32
    )
    input_slice = lax.psum_scatter(input_part, "expert", scatter_dimension=1, tiled=True)
    stat_total = lax.psum(statistic, "expert")
    slice_width = input_slice.shape[1]
    back_input, back_stat = (
        lax.all_to_all(
            input_slice.reshape(groups, capacity, slice_width),
            "node",
            split_axis=0,
            concat_axis=0,
            tiled=True,
        ),
        lax.all_to_all(
            stat_total.reshape(groups, capacity), "node", split_axis=0, concat_axis=0, tiled=True
        ),
    )
    flat_input = back_input.reshape(total_rows, slice_width)
    flat_stat = back_stat.reshape(total_rows)
    flat_index = expert_ids * capacity + jnp.take_along_axis(position, expert_ids, axis=1)
    grad_in = (flat_input[flat_index[:, 0]] + flat_input[flat_index[:, 1]]).astype(jnp.bfloat16)
    grad_gates = flat_stat[flat_index]
    return (grad_in, grad_gates, grad_gate[None], grad_up[None], grad_down[None])


def local(hidden_in, *rest):
    if (lax.axis_size("node"), lax.axis_size("expert")) == (4, 4) and hidden_in.shape[1] % 128 == 0:
        return fast_local(hidden_in, *rest)
    return general_local(hidden_in, *rest)


def solution(mesh):
    return jax.shard_map(
        local,
        mesh=mesh,
        in_specs=(
            P(("parts", "node"), "expert"),
            P(("parts", "node"), "expert"),
            P(("parts", "node"), None),
            P(("parts", "node"), None),
            P("node", "expert", None),
            P("node", "expert", None),
            P("node", "expert", None),
        ),
        out_specs=(
            P(("parts", "node"), "expert"),
            P(("parts", "node"), None),
            P(("parts", "node"), "expert", None),
            P(("parts", "node"), "expert", None),
            P(("parts", "node"), "expert", None),
        ),
        check_vma=False,
    )
```

```python
import functools

import jax
import jax.numpy as jnp
from jax import lax
from jax.experimental import pallas as pl
from jax.experimental.pallas import tpu as pltpu
from jax.sharding import PartitionSpec as P

BF16 = jnp.bfloat16
F32 = jnp.float32
MIB = 1 << 20


def dot_nt(left, right):
    return lax.dot_general(left, right, (((1,), (1,)), ((), ())), preferred_element_type=F32)


def dot_tn(left, right):
    return lax.dot_general(left, right, (((0,), (0,)), ((), ())), preferred_element_type=F32)


def dot_nn(left, right):
    return lax.dot_general(left, right, (((1,), (0,)), ((), ())), preferred_element_type=F32)


def call(kernel, outs, *args, flops=0, nbytes=0, vmem=6 * MIB, scratch=(), in_hbm=()):
    args = [
        pltpu.with_memory_space_constraint(a, pltpu.HBM) if i in in_hbm else a for i, a in enumerate(args)
    ]
    return pl.pallas_call(
        kernel,
        out_shape=outs,
        in_specs=[
            pl.BlockSpec(memory_space=pltpu.HBM if i in in_hbm else pltpu.VMEM) for i in range(len(args))
        ],
        out_specs=[pl.BlockSpec(memory_space=pltpu.VMEM)] * len(outs),
        scratch_shapes=list(scratch),
        compiler_params=pltpu.CompilerParams(vmem_limit_bytes=vmem),
        cost_estimate=pl.CostEstimate(flops=flops, bytes_accessed=nbytes, transcendentals=0),
    )(*args)


def slots_of(ids, expert, capacity):
    tokens = ids.shape[1]
    routed = jnp.max((ids == expert).astype(F32), axis=0, keepdims=True)
    before = (
        lax.broadcasted_iota(jnp.int32, (tokens, tokens), 0)
        < lax.broadcasted_iota(jnp.int32, (tokens, tokens), 1)
    ).astype(BF16)
    position = dot_nn(jnp.broadcast_to(routed, (8, tokens)).astype(BF16), before)[0:1]
    slot = lax.broadcasted_iota(jnp.int32, (capacity, tokens), 0).astype(F32)
    return jnp.where((slot == position) & (routed > 0.0), 1.0, 0.0)


def pack_kernel(groups, *refs):
    sources, outs, local, sems = refs[:4], refs[4 : 4 + groups], refs[4 + groups : 8 + groups], refs[-1]
    copies = [pltpu.make_async_copy(a, b, sems.at[i]) for i, (a, b) in enumerate(zip(sources, local))]
    for copy in copies:
        copy.start()
    ids_ref, gates_ref, hidden_ref, grad_ref = local
    me = lax.axis_index("node")
    copies[0].wait()
    copies[1].wait()
    ids = ids_ref[...]
    capacity = ids.shape[1] // 2
    one_hots = [slots_of(ids, me ^ shift, capacity) for shift in range(groups)]
    copies[2].wait()
    for one_hot, out in zip(one_hots, outs):
        out[:capacity] = dot_nn(one_hot.astype(BF16), hidden_ref[...]).astype(BF16)
    gates = gates_ref[...].astype(F32)
    copies[3].wait()
    for shift, (one_hot, out) in enumerate(zip(one_hots, outs)):
        weight = jnp.sum(jnp.where(ids == (me ^ shift), gates, 0.0), axis=0, keepdims=True)
        out[capacity:] = dot_nn((one_hot * weight).astype(BF16), grad_ref[...]).astype(BF16)


def pick_kernel(groups, ids_ref, out_ref):
    me = lax.axis_index("node")
    ids = ids_ref[...]
    capacity = ids.shape[1] // 2
    for shift in range(groups):
        chosen = slots_of(ids, me ^ shift, capacity)
        out_ref[:, shift * capacity : (shift + 1) * capacity] = chosen.T.astype(BF16)


def load_kernel(*refs):
    count = len(refs) // 2
    sources, outs, sems = refs[:count], refs[count : 2 * count], refs[-1]
    copies = [pltpu.make_async_copy(a, b, sems.at[i]) for i, (a, b) in enumerate(zip(sources, outs))]
    for copy in copies:
        copy.start()
    for copy in copies:
        copy.wait()


def assemble(parts, relatives, groups, base, rows_ref, grads_ref):
    me = lax.axis_index("expert")
    capacity, width = parts[0].shape[0] // 2, parts[0].shape[1]
    for index, part in enumerate(parts):
        place, shift = divmod(index, groups)
        columns = pl.ds(pl.multiple_of(((me ^ relatives[place]) - base) * width, width), width)
        rows = slice(shift * capacity, (shift + 1) * capacity)
        rows_ref[rows, columns] = part[:capacity]
        grads_ref[rows, columns] = part[capacity:]


def local_kernel(groups, *refs):
    parts = refs[: 2 * groups]
    gate_w, up_w, down_w, gate_ref, up_ref, back_ref, rows_ref, grads_ref = refs[2 * groups :]
    base = (lax.axis_index("expert") // 2) * 2
    assemble(parts, (0, 1), groups, base, rows_ref, grads_ref)
    half = rows_ref.shape[1]
    columns = pl.ds(pl.multiple_of(base * (half // 2), half), half)
    gate_ref[...] = dot_nt(gate_w[0, :, columns], rows_ref[...])
    up_ref[...] = dot_nt(up_w[0, :, columns], rows_ref[...])
    back_ref[...] = dot_nt(down_w[0, :, columns], grads_ref[...])


def middle_kernel(groups, *refs):
    parts = refs[: 4 * groups]
    (gate_w, up_w, down_w, gate_ref, up_ref, back_ref,
     rows_ref, grads_ref, dgate_ref, dup_ref, hid_ref, stat_ref) = refs[4 * groups :]
    assemble(parts, (2, 3, 0, 1), groups, 0, rows_ref, grads_ref)
    half = rows_ref.shape[1] // 2
    columns = pl.ds(pl.multiple_of((1 - lax.axis_index("expert") // 2) * half, half), half)
    gate = gate_ref[...] + dot_nt(gate_w[0, :, columns], rows_ref[:, columns])
    up = up_ref[...] + dot_nt(up_w[0, :, columns], rows_ref[:, columns])
    back = back_ref[...] + dot_nt(down_w[0, :, columns], grads_ref[:, columns])
    sig = 1.0 / (1.0 + jnp.exp(-gate))
    silu = gate * sig
    hidden = silu * up
    stat_ref[...] = jnp.broadcast_to(jnp.sum(hidden * back, axis=0, keepdims=True), stat_ref.shape)
    dgate_ref[...] = (back * up * sig * (1.0 + gate * (1.0 - sig))).astype(BF16)
    dup_ref[...] = (back * silu).astype(BF16)
    hid_ref[...] = hidden.astype(BF16)


EXTRA = 8


def halves_of(row):
    high = row.astype(BF16).astype(F32)
    index = lax.broadcasted_iota(jnp.int32, (EXTRA, row.shape[1]), 0)
    return jnp.where(index == 0, high, jnp.where(index == 1, row - high, 0.0)).astype(BF16)


def row_of(halves):
    return halves[0:1].astype(F32) + halves[1:2].astype(F32)


def input_kernel(relative, dgate_ref, dup_ref, gate_w, up_w, stat_ref, out_ref):
    me = lax.axis_index("expert")
    rows, width = dgate_ref.shape[1], out_ref.shape[1]
    columns = pl.ds(pl.multiple_of((me ^ relative) * width, width), width)
    total = dot_tn(dgate_ref[...], gate_w[0, :, columns]) + dot_tn(dup_ref[...], up_w[0, :, columns])
    out_ref[:rows] = total.astype(out_ref.dtype)
    if out_ref.shape[0] > rows:
        out_ref[rows:, :rows] = halves_of(stat_ref[0:1])
        out_ref[rows:, rows:] = jnp.zeros((EXTRA, width - rows), BF16)


def add_kernel(groups, keep, got, stat_ref, *outs):
    capacity = outs[0].shape[0] - EXTRA
    rows = groups * capacity
    stat = stat_ref[0:1] + row_of(got[rows:, :rows])
    outs[groups][...] = jnp.broadcast_to(stat, outs[groups].shape)
    for shift in range(groups):
        block = slice(shift * capacity, (shift + 1) * capacity)
        outs[shift][:capacity] = (keep[block] + got[block].astype(F32)).astype(BF16)
        outs[shift][capacity:, :capacity] = halves_of(stat[:, block])
        outs[shift][capacity:, capacity:] = jnp.zeros((EXTRA, outs[shift].shape[1] - capacity), BF16)


def join_kernel(shift, keep, got, crossed, stat_ref, *rest):
    out = rest[-1]
    capacity = out.shape[0] - EXTRA
    block = slice(shift * capacity, (shift + 1) * capacity)
    out[:capacity] = (keep[block] + got[block].astype(F32) + crossed[:capacity].astype(F32)).astype(BF16)
    out[capacity:, :capacity] = halves_of(stat_ref[0:1, block] + row_of(crossed[capacity:, :capacity]))
    out[capacity:, capacity:] = jnp.zeros((EXTRA, out.shape[1] - capacity), BF16)


def grad_kernel(tile, left_ref, rows_ref, out_ref, mark_ref, held_ref, sems):
    copies = []
    for index in range(rows_ref.shape[1] // tile):
        columns = slice(index * tile, (index + 1) * tile)
        held_ref[:, columns] = dot_nn(left_ref[...], rows_ref[:, columns]).astype(BF16)
        copies.append(pltpu.make_async_copy(held_ref.at[:, columns], out_ref.at[0, :, columns], sems.at[index]))
        copies[-1].start()
    mark_ref[...] = jnp.zeros(mark_ref.shape, F32)
    for copy in copies:
        copy.wait()


def weight_grad(left, rows):
    units, features = left.shape[0], rows.shape[1]
    tile = 512 if features % 512 == 0 else features
    return pl.pallas_call(
        functools.partial(grad_kernel, tile),
        out_shape=[jax.ShapeDtypeStruct((1, units, features), BF16), jax.ShapeDtypeStruct((8, 128), F32)],
        in_specs=[pl.BlockSpec(memory_space=pltpu.VMEM)] * 2,
        out_specs=[pl.BlockSpec(memory_space=pltpu.HBM), pl.BlockSpec(memory_space=pltpu.VMEM)],
        scratch_shapes=[pltpu.VMEM((units, features), BF16), pltpu.SemaphoreType.DMA((features // tile,))],
        compiler_params=pltpu.CompilerParams(vmem_limit_bytes=10 * MIB),
        cost_estimate=pl.CostEstimate(flops=0, bytes_accessed=0, transcendentals=0),
    )(left, rows)


def finish_kernel(groups, ids_ref, gates_in_ref, pick_ref, *refs):
    parts = refs[:groups]
    grad_ref, gates_ref, rows_ref = refs[groups:]
    me = lax.axis_index("node")
    ids = ids_ref[...]
    capacity = ids.shape[1] // 2
    for shift in range(groups):
        rows_ref[shift * capacity : (shift + 1) * capacity] = parts[shift][:capacity]
    grad_ref[...] = dot_nn(pick_ref[...], rows_ref[...]).astype(BF16)
    gates = jnp.zeros(ids.shape, F32)
    for shift in range(groups):
        columns = slice(shift * capacity, (shift + 1) * capacity)
        halves = dot_nt(parts[shift][capacity:, :capacity], pick_ref[:, columns])
        gates = gates + jnp.where(ids == (me ^ shift), halves[0:1] + halves[1:2], 0.0)
    gates_ref[...] = gates / gates_in_ref[...].astype(F32)


def fast_local(hidden_in, out_grad, expert_ids, gate_weights, w_gate, w_up, w_down):
    groups = lax.axis_size("node")
    experts = lax.axis_size("expert")
    tokens, width = hidden_in.shape
    capacity = tokens // 2
    rows = groups * capacity
    units, features = w_gate.shape[1:]
    shape = jax.ShapeDtypeStruct
    after = lax.optimization_barrier

    def over_node(x, shift):
        return lax.ppermute(x, "node", [(i, i ^ shift) for i in range(groups)])

    def over_expert(x, relative):
        return lax.ppermute(x, "expert", [(i, i ^ relative) for i in range(experts)])

    ids, gates = expert_ids.T, gate_weights.T
    blocks = call(
        functools.partial(pack_kernel, groups),
        [shape((tokens, width), BF16)] * groups,
        ids, gates, hidden_in, out_grad,
        flops=4 * rows * tokens * width, nbytes=6 * tokens * width, in_hbm=(0, 1, 2, 3),
        scratch=[
            pltpu.VMEM(ids.shape, ids.dtype), pltpu.VMEM(gates.shape, gates.dtype),
            pltpu.VMEM((tokens, width), BF16), pltpu.VMEM((tokens, width), BF16), pltpu.SemaphoreType.DMA((4,)),
        ],
    )
    own = list(blocks)
    partner, other = [None] * groups, [None] * groups
    other[0] = over_expert(own[0], 2)
    partner[0] = over_expert(own[0], 1)
    own[3] = over_node(blocks[3], 3)
    partner[3] = over_expert(own[3], 1)
    own[2] = over_node(blocks[2], 2)
    partner[2] = over_expert(own[2], 1)
    own[1] = over_node(blocks[1], 1)
    partner[1] = over_expert(own[1], 1)
    mats = after((w_gate, w_up, w_down, partner[0]))[:3]
    mats = call(load_kernel, [shape(m.shape, BF16) for m in mats], *mats, nbytes=12 * units * features,
                in_hbm=(0, 1, 2), scratch=[pltpu.SemaphoreType.DMA((3,))])
    other[1] = over_expert(after((own[1], other[0], mats[0]))[0], 2)
    other[2] = over_expert(after((own[2], mats[0]))[0], 2)
    other[3] = over_expert(after((own[3], other[2]))[0], 2)
    across = [over_expert(x, 1) for x in other[:-1]]

    dense = 2 * rows * units * features
    partial_sums = call(
        functools.partial(local_kernel, groups),
        [shape((units, rows), F32)] * 3,
        *own, *partner, *mats, flops=3 * dense // 2, nbytes=3 * units * features,
        scratch=[pltpu.VMEM((rows, 2 * width), BF16)] * 2,
    )
    across.append(over_expert(after((other[-1], partial_sums[0]))[0], 1))
    rows_in, rows_grad, dgate, dup, hid, stat = call(
        functools.partial(middle_kernel, groups),
        [shape((rows, features), BF16)] * 2 + [shape((units, rows), BF16)] * 3 + [shape((8, rows), F32)],
        *other, *across, *own, *partner, *mats, *partial_sums,
        flops=3 * dense // 2, nbytes=3 * units * features,
    )

    def input_part(relative, extra, kind):
        return call(
            functools.partial(input_kernel, relative), [shape((rows + extra, width), kind)],
            dgate, dup, mats[0], mats[1], stat, flops=dense // 2, nbytes=units * features,
        )[0]

    far_got = over_expert(input_part(3, EXTRA, BF16), 1)
    far_keep = input_part(2, 0, F32)
    *far_sum, stat_pair = call(
        functools.partial(add_kernel, groups),
        [shape((capacity + EXTRA, width), BF16)] * groups + [shape((8, rows), F32)],
        far_keep, far_got, stat, nbytes=6 * rows * width,
    )
    near_got = over_expert(input_part(1, 0, BF16), 1)
    near_keep = input_part(0, 0, F32)
    crossed = [over_expert(x, 2) for x in far_sum]
    lefts = [(dgate, rows_in), (dup, rows_in), (hid, rows_grad)]
    back, totals, marks = [None] * groups, [None] * groups, [None] * groups
    weight_grads = [None] * 3
    totals[3] = call(functools.partial(join_kernel, 3), [shape((capacity + EXTRA, width), BF16)],
                     near_keep, near_got, crossed[3], stat_pair)[0]
    back[3] = over_node(totals[3], 3)
    weight_grads[0], marks[0] = weight_grad(after((dgate, far_sum[0]))[0], rows_in)
    totals[2] = call(functools.partial(join_kernel, 2), [shape((capacity + EXTRA, width), BF16)],
                     near_keep, near_got, crossed[2], stat_pair, marks[0])[0]
    back[2] = over_node(totals[2], 2)
    totals[1] = call(functools.partial(join_kernel, 1), [shape((capacity + EXTRA, width), BF16)],
                     near_keep, near_got, crossed[1], stat_pair, marks[0])[0]
    back[1] = over_node(totals[1], 1)
    weight_grads[1], marks[1] = weight_grad(after((dup, totals[1], totals[2], totals[3]))[0], rows_in)
    totals[0] = call(functools.partial(join_kernel, 0), [shape((capacity + EXTRA, width), BF16)],
                     near_keep, near_got, crossed[0], stat_pair, marks[1])[0]
    back[0] = totals[0]
    weight_grads[2], marks[2] = weight_grad(after((hid, back[3]))[0], rows_grad)

    pick = call(functools.partial(pick_kernel, groups), [shape((tokens, rows), BF16)], after((ids, own[1]))[0])[0]
    grad_in, grad_gates = call(
        functools.partial(finish_kernel, groups),
        [shape((tokens, width), BF16), shape(ids.shape, F32)],
        ids, gates, pick, *back, scratch=[pltpu.VMEM((rows, width), BF16)],
    )
    return (grad_in, grad_gates.T, *weight_grads)


def contract_rows(left, right):
    return lax.dot_general(
        left, right, (((0,), (0,)), ((), ())), preferred_element_type=jnp.float32
    )


def contract_cols(left, right):
    return lax.dot_general(
        left, right, (((1,), (1,)), ((), ())), preferred_element_type=jnp.float32
    )


def expert_backward(rows_in, rows_grad, row_weight, gate_mat, up_mat, down_mat):
    gate_pre = contract_cols(rows_in, gate_mat)
    up_pre = contract_cols(rows_in, up_mat)
    sigmoid_gate = jax.nn.sigmoid(gate_pre)
    silu_gate = gate_pre * sigmoid_gate
    hidden = silu_gate * up_pre
    back_hidden = contract_cols(rows_grad, down_mat)
    statistic = jnp.sum(hidden * back_hidden, axis=1)
    scaled = row_weight[:, None] * back_hidden
    grad_gate_pre = (
        scaled * up_pre * sigmoid_gate * (1.0 + gate_pre * (1.0 - sigmoid_gate))
    ).astype(jnp.bfloat16)
    grad_up_pre = (scaled * silu_gate).astype(jnp.bfloat16)
    weighted_hidden = (row_weight[:, None] * hidden).astype(jnp.bfloat16)
    grad_down = contract_rows(weighted_hidden, rows_grad).astype(jnp.bfloat16)
    grad_gate = contract_rows(grad_gate_pre, rows_in).astype(jnp.bfloat16)
    grad_up = contract_rows(grad_up_pre, rows_in).astype(jnp.bfloat16)
    return (grad_gate, grad_up, grad_down, grad_gate_pre, grad_up_pre, statistic)


def general_local(hidden_in, out_grad, expert_ids, gate_weights, w_gate, w_up, w_down):
    groups = lax.axis_size("node")
    count_tok = hidden_in.shape[0]
    capacity = count_tok // 2
    group_ids = jnp.arange(groups, dtype=jnp.int32)
    member = expert_ids[:, :, None] == group_ids[None, None, :]
    routed = jnp.any(member, axis=1)
    routed_int = routed.astype(jnp.int32)
    position = jnp.cumsum(routed_int, axis=0) - routed_int
    weight_of = jnp.sum(
        jnp.where(member, gate_weights[:, :, None].astype(jnp.float32), jnp.float32(0.0)), axis=1
    )
    slot_ids = jnp.arange(capacity, dtype=jnp.int32)
    landing = routed[:, :, None] & (position[:, :, None] == slot_ids[None, None, :])
    token_of = jnp.sum(
        jnp.where(landing, jnp.arange(count_tok, dtype=jnp.int32)[:, None, None], 0), axis=0
    )
    filled = jnp.any(landing, axis=0)
    send_weight = jnp.where(
        filled, weight_of[token_of, group_ids[:, None]], jnp.float32(0.0)
    ).astype(jnp.bfloat16)

    def pack_rows(source):
        return jnp.where(filled[:, :, None], source[token_of], jnp.zeros((), source.dtype))

    slice_in, slice_grad, recv_weight = (
        lax.all_to_all(pack_rows(hidden_in), "node", split_axis=0, concat_axis=0, tiled=True),
        lax.all_to_all(pack_rows(out_grad), "node", split_axis=0, concat_axis=0, tiled=True),
        lax.all_to_all(send_weight, "node", split_axis=0, concat_axis=0, tiled=True),
    )
    rows_in, rows_grad = (
        lax.all_gather(slice_in, "expert", axis=2, tiled=True),
        lax.all_gather(slice_grad, "expert", axis=2, tiled=True),
    )
    total_rows = groups * capacity
    features = rows_in.shape[2]
    row_weight = recv_weight.reshape(total_rows).astype(jnp.float32)
    gate_mat = w_gate[0]
    up_mat = w_up[0]
    grad_gate, grad_up, grad_down, grad_gate_pre, grad_up_pre, statistic = expert_backward(
        rows_in.reshape(total_rows, features),
        rows_grad.reshape(total_rows, features),
        row_weight,
        gate_mat,
        up_mat,
        w_down[0],
    )
    input_part = jnp.dot(grad_gate_pre, gate_mat, preferred_element_type=jnp.float32) + jnp.dot(
        grad_up_pre, up_mat, preferred_element_type=jnp.float32
    )
    input_slice = lax.psum_scatter(input_part, "expert", scatter_dimension=1, tiled=True)
    stat_total = lax.psum(statistic, "expert")
    slice_width = input_slice.shape[1]
    back_input, back_stat = (
        lax.all_to_all(
            input_slice.reshape(groups, capacity, slice_width),
            "node",
            split_axis=0,
            concat_axis=0,
            tiled=True,
        ),
        lax.all_to_all(
            stat_total.reshape(groups, capacity), "node", split_axis=0, concat_axis=0, tiled=True
        ),
    )
    flat_input = back_input.reshape(total_rows, slice_width)
    flat_stat = back_stat.reshape(total_rows)
    flat_index = expert_ids * capacity + jnp.take_along_axis(position, expert_ids, axis=1)
    grad_in = (flat_input[flat_index[:, 0]] + flat_input[flat_index[:, 1]]).astype(jnp.bfloat16)
    grad_gates = flat_stat[flat_index]
    return (grad_in, grad_gates, grad_gate[None], grad_up[None], grad_down[None])


def local(hidden_in, *rest):
    if (lax.axis_size("node"), lax.axis_size("expert")) == (4, 4) and hidden_in.shape[1] % 128 == 0:
        return fast_local(hidden_in, *rest)
    return general_local(hidden_in, *rest)


def solution(mesh):
    return jax.shard_map(
        local,
        mesh=mesh,
        in_specs=(
            P(("parts", "node"), "expert"),
            P(("parts", "node"), "expert"),
            P(("parts", "node"), None),
            P(("parts", "node"), None),
            P("node", "expert", None),
            P("node", "expert", None),
            P("node", "expert", None),
        ),
        out_specs=(
            P(("parts", "node"), "expert"),
            P(("parts", "node"), None),
            P(("parts", "node"), "expert", None),
            P(("parts", "node"), "expert", None),
            P(("parts", "node"), "expert", None),
        ),
        check_vma=False,
    )
```

```python
import functools

import jax
import jax.numpy as jnp
from jax import lax
from jax.experimental import pallas as pl
from jax.experimental.pallas import tpu as pltpu
from jax.sharding import PartitionSpec as P

BF16 = jnp.bfloat16
F32 = jnp.float32
MIB = 1 << 20


def dot_nt(left, right):
    return lax.dot_general(left, right, (((1,), (1,)), ((), ())), preferred_element_type=F32)


def dot_tn(left, right):
    return lax.dot_general(left, right, (((0,), (0,)), ((), ())), preferred_element_type=F32)


def dot_nn(left, right):
    return lax.dot_general(left, right, (((1,), (0,)), ((), ())), preferred_element_type=F32)


def call(kernel, outs, *args, flops=0, nbytes=0, vmem=6 * MIB, scratch=(), in_hbm=()):
    args = [
        pltpu.with_memory_space_constraint(a, pltpu.HBM) if i in in_hbm else a for i, a in enumerate(args)
    ]
    return pl.pallas_call(
        kernel,
        out_shape=outs,
        in_specs=[
            pl.BlockSpec(memory_space=pltpu.HBM if i in in_hbm else pltpu.VMEM) for i in range(len(args))
        ],
        out_specs=[pl.BlockSpec(memory_space=pltpu.VMEM)] * len(outs),
        scratch_shapes=list(scratch),
        compiler_params=pltpu.CompilerParams(vmem_limit_bytes=vmem),
        cost_estimate=pl.CostEstimate(flops=flops, bytes_accessed=nbytes, transcendentals=0),
    )(*args)


def slots_of(ids, expert, capacity):
    tokens = ids.shape[1]
    routed = jnp.max((ids == expert).astype(F32), axis=0, keepdims=True)
    before = (
        lax.broadcasted_iota(jnp.int32, (tokens, tokens), 0)
        < lax.broadcasted_iota(jnp.int32, (tokens, tokens), 1)
    ).astype(BF16)
    position = dot_nn(jnp.broadcast_to(routed, (8, tokens)).astype(BF16), before)[0:1]
    slot = lax.broadcasted_iota(jnp.int32, (capacity, tokens), 0).astype(F32)
    return jnp.where((slot == position) & (routed > 0.0), 1.0, 0.0)


def pack_kernel(groups, *refs):
    sources, outs, local, sems = refs[:4], refs[4 : 4 + groups], refs[4 + groups : 8 + groups], refs[-1]
    copies = [pltpu.make_async_copy(a, b, sems.at[i]) for i, (a, b) in enumerate(zip(sources, local))]
    for copy in copies:
        copy.start()
    ids_ref, gates_ref, hidden_ref, grad_ref = local
    me = lax.axis_index("node")
    copies[0].wait()
    copies[1].wait()
    ids = ids_ref[...]
    capacity = ids.shape[1] // 2
    one_hots = [slots_of(ids, me ^ shift, capacity) for shift in range(groups)]
    copies[2].wait()
    for one_hot, out in zip(one_hots, outs):
        out[:capacity] = dot_nn(one_hot.astype(BF16), hidden_ref[...]).astype(BF16)
    gates = gates_ref[...].astype(F32)
    copies[3].wait()
    for shift, (one_hot, out) in enumerate(zip(one_hots, outs)):
        weight = jnp.sum(jnp.where(ids == (me ^ shift), gates, 0.0), axis=0, keepdims=True)
        out[capacity:] = dot_nn((one_hot * weight).astype(BF16), grad_ref[...]).astype(BF16)


def pick_kernel(groups, ids_ref, out_ref):
    me = lax.axis_index("node")
    ids = ids_ref[...]
    capacity = ids.shape[1] // 2
    for shift in range(groups):
        chosen = slots_of(ids, me ^ shift, capacity)
        out_ref[:, shift * capacity : (shift + 1) * capacity] = chosen.T.astype(BF16)


def load_kernel(*refs):
    count = len(refs) // 2
    sources, outs, sems = refs[:count], refs[count : 2 * count], refs[-1]
    copies = [pltpu.make_async_copy(a, b, sems.at[i]) for i, (a, b) in enumerate(zip(sources, outs))]
    for copy in copies:
        copy.start()
    for copy in copies:
        copy.wait()


def assemble(parts, relatives, groups, base, rows_ref, grads_ref):
    me = lax.axis_index("expert")
    capacity, width = parts[0].shape[0] // 2, parts[0].shape[1]
    for index, part in enumerate(parts):
        place, shift = divmod(index, groups)
        columns = pl.ds(pl.multiple_of(((me ^ relatives[place]) - base) * width, width), width)
        rows = slice(shift * capacity, (shift + 1) * capacity)
        rows_ref[rows, columns] = part[:capacity]
        grads_ref[rows, columns] = part[capacity:]


def local_kernel(groups, *refs):
    parts = refs[: 2 * groups]
    gate_w, up_w, down_w, gate_ref, up_ref, back_ref, rows_ref, grads_ref = refs[2 * groups :]
    base = (lax.axis_index("expert") // 2) * 2
    assemble(parts, (0, 1), groups, base, rows_ref, grads_ref)
    half = rows_ref.shape[1]
    columns = pl.ds(pl.multiple_of(base * (half // 2), half), half)
    gate_ref[...] = dot_nt(gate_w[0, :, columns], rows_ref[...])
    up_ref[...] = dot_nt(up_w[0, :, columns], rows_ref[...])
    back_ref[...] = dot_nt(down_w[0, :, columns], grads_ref[...])


def with_slice(relative, groups, parts, mats, sums, rows_ref, grads_ref):
    slot = lax.axis_index("expert") ^ relative
    assemble(parts, (relative,), groups, slot, rows_ref, grads_ref)
    width = rows_ref.shape[1]
    columns = pl.ds(pl.multiple_of(slot * width, width), width)
    rights = (rows_ref, rows_ref, grads_ref)
    return [total[...] + dot_nt(mat[0, :, columns], right[...]) for total, mat, right in zip(sums, mats, rights)]


def side_kernel(groups, *refs):
    parts, mats, sums, outs = refs[:groups], refs[groups : groups + 3], refs[groups + 3 : groups + 6], refs[-5:]
    for out, value in zip(outs, with_slice(2, groups, parts, mats, sums, *outs[3:])):
        out[...] = value


def middle_kernel(groups, *refs):
    parts, mats, sums = refs[:groups], refs[groups : groups + 3], refs[groups + 3 : groups + 6]
    rows_ref, grads_ref, dgate_ref, dup_ref, hid_ref, stat_ref = refs[groups + 6 :]
    gate, up, back = with_slice(3, groups, parts, mats, sums, rows_ref, grads_ref)
    sig = 1.0 / (1.0 + jnp.exp(-gate))
    silu = gate * sig
    hidden = silu * up
    stat_ref[...] = jnp.broadcast_to(jnp.sum(hidden * back, axis=0, keepdims=True), stat_ref.shape)
    dgate_ref[...] = (back * up * sig * (1.0 + gate * (1.0 - sig))).astype(BF16)
    dup_ref[...] = (back * silu).astype(BF16)
    hid_ref[...] = hidden.astype(BF16)


EXTRA = 8


def halves_of(row):
    high = row.astype(BF16).astype(F32)
    index = lax.broadcasted_iota(jnp.int32, (EXTRA, row.shape[1]), 0)
    return jnp.where(index == 0, high, jnp.where(index == 1, row - high, 0.0)).astype(BF16)


def row_of(halves):
    return halves[0:1].astype(F32) + halves[1:2].astype(F32)


def input_kernel(relative, dgate_ref, dup_ref, gate_w, up_w, stat_ref, out_ref):
    me = lax.axis_index("expert")
    rows, width = dgate_ref.shape[1], out_ref.shape[1]
    columns = pl.ds(pl.multiple_of((me ^ relative) * width, width), width)
    total = dot_tn(dgate_ref[...], gate_w[0, :, columns]) + dot_tn(dup_ref[...], up_w[0, :, columns])
    out_ref[:rows] = total.astype(out_ref.dtype)
    if out_ref.shape[0] > rows:
        out_ref[rows:, :rows] = halves_of(stat_ref[0:1])
        out_ref[rows:, rows:] = jnp.zeros((EXTRA, width - rows), BF16)


def add_kernel(groups, keep, got, stat_ref, *outs):
    capacity = outs[0].shape[0] - EXTRA
    rows = groups * capacity
    stat = stat_ref[0:1] + row_of(got[rows:, :rows])
    outs[groups][...] = jnp.broadcast_to(stat, outs[groups].shape)
    for shift in range(groups):
        block = slice(shift * capacity, (shift + 1) * capacity)
        outs[shift][:capacity] = (keep[block] + got[block].astype(F32)).astype(BF16)
        outs[shift][capacity:, :capacity] = halves_of(stat[:, block])
        outs[shift][capacity:, capacity:] = jnp.zeros((EXTRA, outs[shift].shape[1] - capacity), BF16)


def join_kernel(shift, keep, got, crossed, stat_ref, *rest):
    out = rest[-1]
    capacity = out.shape[0] - EXTRA
    block = slice(shift * capacity, (shift + 1) * capacity)
    out[:capacity] = (keep[block] + got[block].astype(F32) + crossed[:capacity].astype(F32)).astype(BF16)
    out[capacity:, :capacity] = halves_of(stat_ref[0:1, block] + row_of(crossed[capacity:, :capacity]))
    out[capacity:, capacity:] = jnp.zeros((EXTRA, out.shape[1] - capacity), BF16)


def grad_kernel(tiles, left_ref, local_ref, other_ref, across_ref, out_ref, mark_ref, held_ref, sems):
    me = lax.axis_index("expert")
    width = other_ref.shape[1]
    pieces = ((local_ref, (me // 2) * 2), (other_ref, me ^ 2), (across_ref, me ^ 3))
    copies, held_from = [], 0
    for index, (piece, start, size) in enumerate(tiles):
        piece_ref, slot = pieces[piece]
        held = held_ref.at[:, held_from : held_from + size]
        held[...] = dot_nn(left_ref[...], piece_ref[:, start : start + size]).astype(BF16)
        columns = pl.ds(pl.multiple_of(slot * width + start, 128), size)
        copies.append(pltpu.make_async_copy(held, out_ref.at[0, :, columns], sems.at[index]))
        copies[-1].start()
        held_from += size
    mark_ref[...] = jnp.zeros(mark_ref.shape, F32)
    for copy in copies:
        copy.wait()


def weight_grad(left, pieces):
    units, features = left.shape[0], sum(piece.shape[1] for piece in pieces)
    tiles = [
        (which, start, min(512, piece.shape[1] - start))
        for which, piece in enumerate(pieces) for start in range(0, piece.shape[1], 512)
    ]
    return pl.pallas_call(
        functools.partial(grad_kernel, tiles),
        out_shape=[jax.ShapeDtypeStruct((1, units, features), BF16), jax.ShapeDtypeStruct((8, 128), F32)],
        in_specs=[pl.BlockSpec(memory_space=pltpu.VMEM)] * 4,
        out_specs=[pl.BlockSpec(memory_space=pltpu.HBM), pl.BlockSpec(memory_space=pltpu.VMEM)],
        scratch_shapes=[pltpu.VMEM((units, features), BF16), pltpu.SemaphoreType.DMA((len(tiles),))],
        compiler_params=pltpu.CompilerParams(vmem_limit_bytes=10 * MIB),
        cost_estimate=pl.CostEstimate(flops=0, bytes_accessed=0, transcendentals=0),
    )(left, *pieces)


def finish_kernel(groups, ids_ref, gates_in_ref, pick_ref, *refs):
    parts = refs[:groups]
    grad_ref, gates_ref, rows_ref = refs[groups:]
    me = lax.axis_index("node")
    ids = ids_ref[...]
    capacity = ids.shape[1] // 2
    for shift in range(groups):
        rows_ref[shift * capacity : (shift + 1) * capacity] = parts[shift][:capacity]
    grad_ref[...] = dot_nn(pick_ref[...], rows_ref[...]).astype(BF16)
    gates = jnp.zeros(ids.shape, F32)
    for shift in range(groups):
        columns = slice(shift * capacity, (shift + 1) * capacity)
        halves = dot_nt(parts[shift][capacity:, :capacity], pick_ref[:, columns])
        gates = gates + jnp.where(ids == (me ^ shift), halves[0:1] + halves[1:2], 0.0)
    gates_ref[...] = gates / gates_in_ref[...].astype(F32)


def fast_local(hidden_in, out_grad, expert_ids, gate_weights, w_gate, w_up, w_down):
    groups = lax.axis_size("node")
    experts = lax.axis_size("expert")
    tokens, width = hidden_in.shape
    capacity = tokens // 2
    rows = groups * capacity
    units, features = w_gate.shape[1:]
    shape = jax.ShapeDtypeStruct
    after = lax.optimization_barrier

    def over_node(x, shift):
        return lax.ppermute(x, "node", [(i, i ^ shift) for i in range(groups)])

    def over_expert(x, relative):
        return lax.ppermute(x, "expert", [(i, i ^ relative) for i in range(experts)])

    ids, gates = expert_ids.T, gate_weights.T
    blocks = call(
        functools.partial(pack_kernel, groups),
        [shape((tokens, width), BF16)] * groups,
        ids, gates, hidden_in, out_grad,
        flops=4 * rows * tokens * width, nbytes=6 * tokens * width, in_hbm=(0, 1, 2, 3),
        scratch=[
            pltpu.VMEM(ids.shape, ids.dtype), pltpu.VMEM(gates.shape, gates.dtype),
            pltpu.VMEM((tokens, width), BF16), pltpu.VMEM((tokens, width), BF16), pltpu.SemaphoreType.DMA((4,)),
        ],
    )
    own = list(blocks)
    partner, other = [None] * groups, [None] * groups
    other[0] = over_expert(own[0], 2)
    partner[0] = over_expert(own[0], 1)
    own[3] = over_node(blocks[3], 3)
    partner[3] = over_expert(own[3], 1)
    own[2] = over_node(blocks[2], 2)
    partner[2] = over_expert(own[2], 1)
    own[1] = over_node(blocks[1], 1)
    partner[1] = over_expert(own[1], 1)
    mats = after((w_gate, w_up, w_down, partner[0]))[:3]
    mats = call(load_kernel, [shape(m.shape, BF16) for m in mats], *mats, nbytes=12 * units * features,
                in_hbm=(0, 1, 2), scratch=[pltpu.SemaphoreType.DMA((3,))])
    other[1] = over_expert(after((own[1], other[0], mats[0]))[0], 2)
    other[2] = over_expert(after((own[2], mats[0]))[0], 2)
    other[3] = over_expert(after((own[3], other[2]))[0], 2)
    across = [over_expert(x, 1) for x in other[:-1]]

    dense = 2 * rows * units * features
    *sums, rows_local, grads_local = call(
        functools.partial(local_kernel, groups),
        [shape((units, rows), F32)] * 3 + [shape((rows, 2 * width), BF16)] * 2,
        *own, *partner, *mats, flops=3 * dense // 2, nbytes=3 * units * features,
    )
    across.append(over_expert(after((other[-1], sums[0]))[0], 1))
    *sums, rows_other, grads_other = call(
        functools.partial(side_kernel, groups),
        [shape((units, rows), F32)] * 3 + [shape((rows, width), BF16)] * 2,
        *other, *mats, *sums, flops=3 * dense // 4, nbytes=3 * units * features // 2,
    )
    rows_across, grads_across, dgate, dup, hid, stat = call(
        functools.partial(middle_kernel, groups),
        [shape((rows, width), BF16)] * 2 + [shape((units, rows), BF16)] * 3 + [shape((8, rows), F32)],
        *across, *mats, *sums, flops=3 * dense // 4, nbytes=3 * units * features // 2,
    )
    rows_in = [rows_local, rows_other, rows_across]
    rows_grad = [grads_local, grads_other, grads_across]

    def input_part(relative, extra, kind):
        return call(
            functools.partial(input_kernel, relative), [shape((rows + extra, width), kind)],
            dgate, dup, mats[0], mats[1], stat, flops=dense // 2, nbytes=units * features,
        )[0]

    far_got = over_expert(input_part(3, EXTRA, BF16), 1)
    far_keep = input_part(2, 0, F32)
    *far_sum, stat_pair = call(
        functools.partial(add_kernel, groups),
        [shape((capacity + EXTRA, width), BF16)] * groups + [shape((8, rows), F32)],
        far_keep, far_got, stat, nbytes=6 * rows * width,
    )
    near_got = over_expert(input_part(1, 0, BF16), 1)
    near_keep = input_part(0, 0, F32)
    crossed = [over_expert(x, 2) for x in far_sum]
    lefts = [(dgate, rows_in), (dup, rows_in), (hid, rows_grad)]
    back, totals, marks = [None] * groups, [None] * groups, [None] * groups
    weight_grads = [None] * 3
    totals[3] = call(functools.partial(join_kernel, 3), [shape((capacity + EXTRA, width), BF16)],
                     near_keep, near_got, crossed[3], stat_pair)[0]
    back[3] = over_node(totals[3], 3)
    weight_grads[0], marks[0] = weight_grad(after((dgate, far_sum[0]))[0], rows_in)
    totals[2] = call(functools.partial(join_kernel, 2), [shape((capacity + EXTRA, width), BF16)],
                     near_keep, near_got, crossed[2], stat_pair, marks[0])[0]
    back[2] = over_node(totals[2], 2)
    totals[1] = call(functools.partial(join_kernel, 1), [shape((capacity + EXTRA, width), BF16)],
                     near_keep, near_got, crossed[1], stat_pair, marks[0])[0]
    back[1] = over_node(totals[1], 1)
    weight_grads[1], marks[1] = weight_grad(after((dup, totals[1], totals[2], totals[3]))[0], rows_in)
    totals[0] = call(functools.partial(join_kernel, 0), [shape((capacity + EXTRA, width), BF16)],
                     near_keep, near_got, crossed[0], stat_pair, marks[1])[0]
    back[0] = totals[0]
    weight_grads[2], marks[2] = weight_grad(after((hid, back[3]))[0], rows_grad)

    pick = call(functools.partial(pick_kernel, groups), [shape((tokens, rows), BF16)], after((ids, own[1]))[0])[0]
    grad_in, grad_gates = call(
        functools.partial(finish_kernel, groups),
        [shape((tokens, width), BF16), shape(ids.shape, F32)],
        ids, gates, pick, *back, scratch=[pltpu.VMEM((rows, width), BF16)],
    )
    return (grad_in, grad_gates.T, *weight_grads)


def contract_rows(left, right):
    return lax.dot_general(
        left, right, (((0,), (0,)), ((), ())), preferred_element_type=jnp.float32
    )


def contract_cols(left, right):
    return lax.dot_general(
        left, right, (((1,), (1,)), ((), ())), preferred_element_type=jnp.float32
    )


def expert_backward(rows_in, rows_grad, row_weight, gate_mat, up_mat, down_mat):
    gate_pre = contract_cols(rows_in, gate_mat)
    up_pre = contract_cols(rows_in, up_mat)
    sigmoid_gate = jax.nn.sigmoid(gate_pre)
    silu_gate = gate_pre * sigmoid_gate
    hidden = silu_gate * up_pre
    back_hidden = contract_cols(rows_grad, down_mat)
    statistic = jnp.sum(hidden * back_hidden, axis=1)
    scaled = row_weight[:, None] * back_hidden
    grad_gate_pre = (
        scaled * up_pre * sigmoid_gate * (1.0 + gate_pre * (1.0 - sigmoid_gate))
    ).astype(jnp.bfloat16)
    grad_up_pre = (scaled * silu_gate).astype(jnp.bfloat16)
    weighted_hidden = (row_weight[:, None] * hidden).astype(jnp.bfloat16)
    grad_down = contract_rows(weighted_hidden, rows_grad).astype(jnp.bfloat16)
    grad_gate = contract_rows(grad_gate_pre, rows_in).astype(jnp.bfloat16)
    grad_up = contract_rows(grad_up_pre, rows_in).astype(jnp.bfloat16)
    return (grad_gate, grad_up, grad_down, grad_gate_pre, grad_up_pre, statistic)


def general_local(hidden_in, out_grad, expert_ids, gate_weights, w_gate, w_up, w_down):
    groups = lax.axis_size("node")
    count_tok = hidden_in.shape[0]
    capacity = count_tok // 2
    group_ids = jnp.arange(groups, dtype=jnp.int32)
    member = expert_ids[:, :, None] == group_ids[None, None, :]
    routed = jnp.any(member, axis=1)
    routed_int = routed.astype(jnp.int32)
    position = jnp.cumsum(routed_int, axis=0) - routed_int
    weight_of = jnp.sum(
        jnp.where(member, gate_weights[:, :, None].astype(jnp.float32), jnp.float32(0.0)), axis=1
    )
    slot_ids = jnp.arange(capacity, dtype=jnp.int32)
    landing = routed[:, :, None] & (position[:, :, None] == slot_ids[None, None, :])
    token_of = jnp.sum(
        jnp.where(landing, jnp.arange(count_tok, dtype=jnp.int32)[:, None, None], 0), axis=0
    )
    filled = jnp.any(landing, axis=0)
    send_weight = jnp.where(
        filled, weight_of[token_of, group_ids[:, None]], jnp.float32(0.0)
    ).astype(jnp.bfloat16)

    def pack_rows(source):
        return jnp.where(filled[:, :, None], source[token_of], jnp.zeros((), source.dtype))

    slice_in, slice_grad, recv_weight = (
        lax.all_to_all(pack_rows(hidden_in), "node", split_axis=0, concat_axis=0, tiled=True),
        lax.all_to_all(pack_rows(out_grad), "node", split_axis=0, concat_axis=0, tiled=True),
        lax.all_to_all(send_weight, "node", split_axis=0, concat_axis=0, tiled=True),
    )
    rows_in, rows_grad = (
        lax.all_gather(slice_in, "expert", axis=2, tiled=True),
        lax.all_gather(slice_grad, "expert", axis=2, tiled=True),
    )
    total_rows = groups * capacity
    features = rows_in.shape[2]
    row_weight = recv_weight.reshape(total_rows).astype(jnp.float32)
    gate_mat = w_gate[0]
    up_mat = w_up[0]
    grad_gate, grad_up, grad_down, grad_gate_pre, grad_up_pre, statistic = expert_backward(
        rows_in.reshape(total_rows, features),
        rows_grad.reshape(total_rows, features),
        row_weight,
        gate_mat,
        up_mat,
        w_down[0],
    )
    input_part = jnp.dot(grad_gate_pre, gate_mat, preferred_element_type=jnp.float32) + jnp.dot(
        grad_up_pre, up_mat, preferred_element_type=jnp.float32
    )
    input_slice = lax.psum_scatter(input_part, "expert", scatter_dimension=1, tiled=True)
    stat_total = lax.psum(statistic, "expert")
    slice_width = input_slice.shape[1]
    back_input, back_stat = (
        lax.all_to_all(
            input_slice.reshape(groups, capacity, slice_width),
            "node",
            split_axis=0,
            concat_axis=0,
            tiled=True,
        ),
        lax.all_to_all(
            stat_total.reshape(groups, capacity), "node", split_axis=0, concat_axis=0, tiled=True
        ),
    )
    flat_input = back_input.reshape(total_rows, slice_width)
    flat_stat = back_stat.reshape(total_rows)
    flat_index = expert_ids * capacity + jnp.take_along_axis(position, expert_ids, axis=1)
    grad_in = (flat_input[flat_index[:, 0]] + flat_input[flat_index[:, 1]]).astype(jnp.bfloat16)
    grad_gates = flat_stat[flat_index]
    return (grad_in, grad_gates, grad_gate[None], grad_up[None], grad_down[None])


def local(hidden_in, *rest):
    if (lax.axis_size("node"), lax.axis_size("expert")) == (4, 4) and hidden_in.shape[1] % 128 == 0:
        return fast_local(hidden_in, *rest)
    return general_local(hidden_in, *rest)


def solution(mesh):
    return jax.shard_map(
        local,
        mesh=mesh,
        in_specs=(
            P(("parts", "node"), "expert"),
            P(("parts", "node"), "expert"),
            P(("parts", "node"), None),
            P(("parts", "node"), None),
            P("node", "expert", None),
            P("node", "expert", None),
            P("node", "expert", None),
        ),
        out_specs=(
            P(("parts", "node"), "expert"),
            P(("parts", "node"), None),
            P(("parts", "node"), "expert", None),
            P(("parts", "node"), "expert", None),
            P(("parts", "node"), "expert", None),
        ),
        check_vma=False,
    )
```

```python
import functools

import jax
import jax.numpy as jnp
from jax import lax
from jax.experimental import pallas as pl
from jax.experimental.pallas import tpu as pltpu
from jax.sharding import PartitionSpec as P

BF16 = jnp.bfloat16
F32 = jnp.float32
MIB = 1 << 20


def dot_nt(left, right):
    return lax.dot_general(left, right, (((1,), (1,)), ((), ())), preferred_element_type=F32)


def dot_tn(left, right):
    return lax.dot_general(left, right, (((0,), (0,)), ((), ())), preferred_element_type=F32)


def dot_nn(left, right):
    return lax.dot_general(left, right, (((1,), (0,)), ((), ())), preferred_element_type=F32)


def call(kernel, outs, *args, flops=0, nbytes=0, vmem=6 * MIB, scratch=(), in_hbm=()):
    args = [
        pltpu.with_memory_space_constraint(a, pltpu.HBM) if i in in_hbm else a for i, a in enumerate(args)
    ]
    return pl.pallas_call(
        kernel,
        out_shape=outs,
        in_specs=[
            pl.BlockSpec(memory_space=pltpu.HBM if i in in_hbm else pltpu.VMEM) for i in range(len(args))
        ],
        out_specs=[pl.BlockSpec(memory_space=pltpu.VMEM)] * len(outs),
        scratch_shapes=list(scratch),
        compiler_params=pltpu.CompilerParams(vmem_limit_bytes=vmem),
        cost_estimate=pl.CostEstimate(flops=flops, bytes_accessed=nbytes, transcendentals=0),
    )(*args)


def slots_of(ids, groups, capacity):
    me = lax.axis_index("node")
    tokens = ids.shape[1]
    row = lax.broadcasted_iota(jnp.int32, (8, tokens), 0)
    expert = jnp.where(row < groups, me ^ row, -1)
    routed = jnp.where((ids[0:1] == expert) | (ids[1:2] == expert), 1.0, 0.0)
    before = (
        lax.broadcasted_iota(jnp.int32, (tokens, tokens), 0)
        < lax.broadcasted_iota(jnp.int32, (tokens, tokens), 1)
    ).astype(BF16)
    position = jnp.where(routed > 0.0, dot_nn(routed.astype(BF16), before), -1.0)
    slot = lax.broadcasted_iota(jnp.int32, (capacity, tokens), 0).astype(F32)
    return [jnp.where(slot == position[shift : shift + 1], 1.0, 0.0) for shift in range(groups)]


def pack_kernel(groups, *refs):
    sources, outs, local, sems = refs[:4], refs[4 : 4 + groups], refs[4 + groups : 8 + groups], refs[-1]
    copies = [pltpu.make_async_copy(a, b, sems.at[i]) for i, (a, b) in enumerate(zip(sources, local))]
    for copy in copies:
        copy.start()
    ids_ref, gates_ref, hidden_ref, grad_ref = local
    me = lax.axis_index("node")
    copies[0].wait()
    copies[1].wait()
    ids = ids_ref[...]
    capacity = ids.shape[1] // 2
    one_hots = slots_of(ids, groups, capacity)
    copies[2].wait()
    for one_hot, out in zip(one_hots, outs):
        out[:capacity] = dot_nn(one_hot.astype(BF16), hidden_ref[...]).astype(BF16)
    gates = gates_ref[...].astype(F32)
    copies[3].wait()
    for shift, (one_hot, out) in enumerate(zip(one_hots, outs)):
        weight = jnp.sum(jnp.where(ids == (me ^ shift), gates, 0.0), axis=0, keepdims=True)
        out[capacity:] = dot_nn((one_hot * weight).astype(BF16), grad_ref[...]).astype(BF16)


def pick_kernel(groups, ids_ref, out_ref):
    ids = ids_ref[...]
    capacity = ids.shape[1] // 2
    for shift, chosen in enumerate(slots_of(ids, groups, capacity)):
        out_ref[:, shift * capacity : (shift + 1) * capacity] = chosen.T.astype(BF16)


def load_kernel(*refs):
    count = len(refs) // 2
    sources, outs, sems = refs[:count], refs[count : 2 * count], refs[-1]
    copies = [pltpu.make_async_copy(a, b, sems.at[i]) for i, (a, b) in enumerate(zip(sources, outs))]
    for copy in copies:
        copy.start()
    for copy in copies:
        copy.wait()


def assemble(parts, relatives, groups, base, rows_ref, grads_ref):
    me = lax.axis_index("expert")
    capacity, width = parts[0].shape[0] // 2, parts[0].shape[1]
    for index, part in enumerate(parts):
        place, shift = divmod(index, groups)
        columns = pl.ds(pl.multiple_of(((me ^ relatives[place]) - base) * width, width), width)
        rows = slice(shift * capacity, (shift + 1) * capacity)
        rows_ref[rows, columns] = part[:capacity]
        grads_ref[rows, columns] = part[capacity:]


def local_kernel(groups, *refs):
    parts = refs[: 2 * groups]
    gate_w, up_w, down_w, gate_ref, up_ref, back_ref, rows_ref, grads_ref = refs[2 * groups :]
    base = (lax.axis_index("expert") // 2) * 2
    assemble(parts, (0, 1), groups, base, rows_ref, grads_ref)
    half = rows_ref.shape[1]
    columns = pl.ds(pl.multiple_of(base * (half // 2), half), half)
    gate_ref[...] = dot_nt(gate_w[0, :, columns], rows_ref[...])
    up_ref[...] = dot_nt(up_w[0, :, columns], rows_ref[...])
    back_ref[...] = dot_nt(down_w[0, :, columns], grads_ref[...])


def with_slice(relative, groups, parts, mats, sums, rows_ref, grads_ref):
    slot = lax.axis_index("expert") ^ relative
    assemble(parts, (relative,), groups, slot, rows_ref, grads_ref)
    width = rows_ref.shape[1]
    columns = pl.ds(pl.multiple_of(slot * width, width), width)
    rights = (rows_ref, rows_ref, grads_ref)
    return [total[...] + dot_nt(mat[0, :, columns], right[...]) for total, mat, right in zip(sums, mats, rights)]


def side_kernel(groups, *refs):
    parts, mats, sums, outs = refs[:groups], refs[groups : groups + 3], refs[groups + 3 : groups + 6], refs[-5:]
    for out, value in zip(outs, with_slice(2, groups, parts, mats, sums, *outs[3:])):
        out[...] = value


def middle_kernel(groups, *refs):
    parts, mats, sums = refs[:groups], refs[groups : groups + 3], refs[groups + 3 : groups + 6]
    rows_ref, grads_ref, dgate_ref, dup_ref, hid_ref, stat_ref = refs[groups + 6 :]
    gate, up, back = with_slice(3, groups, parts, mats, sums, rows_ref, grads_ref)
    sig = 1.0 / (1.0 + jnp.exp(-gate))
    silu = gate * sig
    hidden = silu * up
    stat_ref[...] = jnp.broadcast_to(jnp.sum(hidden * back, axis=0, keepdims=True), stat_ref.shape)
    dgate_ref[...] = (back * up * sig * (1.0 + gate * (1.0 - sig))).astype(BF16)
    dup_ref[...] = (back * silu).astype(BF16)
    hid_ref[...] = hidden.astype(BF16)


EXTRA = 8


def halves_of(row):
    high = row.astype(BF16).astype(F32)
    index = lax.broadcasted_iota(jnp.int32, (EXTRA, row.shape[1]), 0)
    return jnp.where(index == 0, high, jnp.where(index == 1, row - high, 0.0)).astype(BF16)


def row_of(halves):
    return halves[0:1].astype(F32) + halves[1:2].astype(F32)


def input_kernel(relative, dgate_ref, dup_ref, gate_w, up_w, stat_ref, out_ref):
    me = lax.axis_index("expert")
    rows, width = dgate_ref.shape[1], out_ref.shape[1]
    columns = pl.ds(pl.multiple_of((me ^ relative) * width, width), width)
    total = dot_tn(dgate_ref[...], gate_w[0, :, columns]) + dot_tn(dup_ref[...], up_w[0, :, columns])
    out_ref[:rows] = total.astype(out_ref.dtype)
    if out_ref.shape[0] > rows:
        out_ref[rows:, :rows] = halves_of(stat_ref[0:1])
        out_ref[rows:, rows:] = jnp.zeros((EXTRA, width - rows), BF16)


def add_kernel(groups, keep, got, stat_ref, *outs):
    capacity = outs[0].shape[0] - EXTRA
    rows = groups * capacity
    stat = stat_ref[0:1] + row_of(got[rows:, :rows])
    outs[groups][...] = jnp.broadcast_to(stat, outs[groups].shape)
    for shift in range(groups):
        block = slice(shift * capacity, (shift + 1) * capacity)
        outs[shift][:capacity] = (keep[block] + got[block].astype(F32)).astype(BF16)
        outs[shift][capacity:, :capacity] = halves_of(stat[:, block])
        outs[shift][capacity:, capacity:] = jnp.zeros((EXTRA, outs[shift].shape[1] - capacity), BF16)


def join_kernel(shift, keep, got, crossed, stat_ref, *rest):
    out = rest[-1]
    capacity = out.shape[0] - EXTRA
    block = slice(shift * capacity, (shift + 1) * capacity)
    out[:capacity] = (keep[block] + got[block].astype(F32) + crossed[:capacity].astype(F32)).astype(BF16)
    out[capacity:, :capacity] = halves_of(stat_ref[0:1, block] + row_of(crossed[capacity:, :capacity]))
    out[capacity:, capacity:] = jnp.zeros((EXTRA, out.shape[1] - capacity), BF16)


def grad_kernel(tiles, left_ref, local_ref, other_ref, across_ref, out_ref, *rest):
    marks, (held_ref, sems) = rest[:-2], rest[-2:]
    me = lax.axis_index("expert")
    width = other_ref.shape[1]
    pieces = ((local_ref, (me // 2) * 2), (other_ref, me ^ 2), (across_ref, me ^ 3))
    copies, held_from = [], 0
    for index, (piece, start, size) in enumerate(tiles):
        piece_ref, slot = pieces[piece]
        held = held_ref.at[:, held_from : held_from + size]
        held[...] = dot_nn(left_ref[...], piece_ref[:, start : start + size]).astype(BF16)
        columns = pl.ds(pl.multiple_of(slot * width + start, 128), size)
        copies.append(pltpu.make_async_copy(held, out_ref.at[0, :, columns], sems.at[index]))
        copies[-1].start()
        held_from += size
    for mark_ref in marks:
        mark_ref[...] = jnp.zeros(mark_ref.shape, F32)
    for copy in copies:
        copy.wait()


def weight_grad(left, pieces, mark=True):
    units, features = left.shape[0], sum(piece.shape[1] for piece in pieces)
    tiles = [
        (which, start, min(512, piece.shape[1] - start))
        for which, piece in enumerate(pieces) for start in range(0, piece.shape[1], 512)
    ]
    return pl.pallas_call(
        functools.partial(grad_kernel, tiles),
        out_shape=[jax.ShapeDtypeStruct((1, units, features), BF16)] + [jax.ShapeDtypeStruct((8, 128), F32)] * mark,
        in_specs=[pl.BlockSpec(memory_space=pltpu.VMEM)] * 4,
        out_specs=[pl.BlockSpec(memory_space=pltpu.HBM)] + [pl.BlockSpec(memory_space=pltpu.VMEM)] * mark,
        scratch_shapes=[pltpu.VMEM((units, features), BF16), pltpu.SemaphoreType.DMA((len(tiles),))],
        compiler_params=pltpu.CompilerParams(vmem_limit_bytes=10 * MIB),
        cost_estimate=pl.CostEstimate(flops=0, bytes_accessed=0, transcendentals=0),
    )(left, *pieces)


def finish_kernel(groups, ids_ref, gates_in_ref, pick_ref, *refs):
    parts = refs[:groups]
    grad_ref, gates_ref, rows_ref = refs[groups:]
    me = lax.axis_index("node")
    ids = ids_ref[...]
    capacity = ids.shape[1] // 2
    for shift in range(groups):
        rows_ref[shift * capacity : (shift + 1) * capacity] = parts[shift][:capacity]
    grad_ref[...] = dot_nn(pick_ref[...], rows_ref[...]).astype(BF16)
    gates = jnp.zeros(ids.shape, F32)
    for shift in range(groups):
        columns = slice(shift * capacity, (shift + 1) * capacity)
        halves = dot_nt(parts[shift][capacity:, :capacity], pick_ref[:, columns])
        gates = gates + jnp.where(ids == (me ^ shift), halves[0:1] + halves[1:2], 0.0)
    gates_ref[...] = gates / gates_in_ref[...].astype(F32)


def fast_local(hidden_in, out_grad, expert_ids, gate_weights, w_gate, w_up, w_down):
    groups = lax.axis_size("node")
    experts = lax.axis_size("expert")
    tokens, width = hidden_in.shape
    capacity = tokens // 2
    rows = groups * capacity
    units, features = w_gate.shape[1:]
    shape = jax.ShapeDtypeStruct
    after = lax.optimization_barrier

    def over_node(x, shift):
        return lax.ppermute(x, "node", [(i, i ^ shift) for i in range(groups)])

    def over_expert(x, relative):
        return lax.ppermute(x, "expert", [(i, i ^ relative) for i in range(experts)])

    ids, gates = expert_ids.T, gate_weights.T
    blocks = call(
        functools.partial(pack_kernel, groups),
        [shape((tokens, width), BF16)] * groups,
        ids, gates, hidden_in, out_grad,
        flops=4 * rows * tokens * width, nbytes=6 * tokens * width, in_hbm=(0, 1, 2, 3),
        scratch=[
            pltpu.VMEM(ids.shape, ids.dtype), pltpu.VMEM(gates.shape, gates.dtype),
            pltpu.VMEM((tokens, width), BF16), pltpu.VMEM((tokens, width), BF16), pltpu.SemaphoreType.DMA((4,)),
        ],
    )
    own = list(blocks)
    partner, other = [None] * groups, [None] * groups
    other[0] = over_expert(own[0], 2)
    partner[0] = over_expert(own[0], 1)
    own[3] = over_node(blocks[3], 3)
    partner[3] = over_expert(own[3], 1)
    own[2] = over_node(blocks[2], 2)
    partner[2] = over_expert(own[2], 1)
    own[1] = over_node(blocks[1], 1)
    partner[1] = over_expert(own[1], 1)
    mats = after((w_gate, w_up, w_down, partner[0]))[:3]
    mats = call(load_kernel, [shape(m.shape, BF16) for m in mats], *mats, nbytes=12 * units * features,
                in_hbm=(0, 1, 2), scratch=[pltpu.SemaphoreType.DMA((3,))])
    other[1] = over_expert(after((own[1], other[0], mats[0]))[0], 2)
    other[2] = over_expert(after((own[2], mats[0]))[0], 2)
    other[3] = over_expert(after((own[3], other[2]))[0], 2)
    across = [over_expert(x, 1) for x in other[:-1]]

    dense = 2 * rows * units * features
    *sums, rows_local, grads_local = call(
        functools.partial(local_kernel, groups),
        [shape((units, rows), F32)] * 3 + [shape((rows, 2 * width), BF16)] * 2,
        *own, *partner, *mats, flops=3 * dense // 2, nbytes=3 * units * features,
    )
    pick = call(functools.partial(pick_kernel, groups), [shape((tokens, rows), BF16)], after((ids, own[1]))[0])[0]
    across.append(over_expert(after((other[-1], sums[0], pick))[0], 1))
    *sums, rows_other, grads_other = call(
        functools.partial(side_kernel, groups),
        [shape((units, rows), F32)] * 3 + [shape((rows, width), BF16)] * 2,
        *other, *mats, *sums, flops=3 * dense // 4, nbytes=3 * units * features // 2,
    )
    rows_across, grads_across, dgate, dup, hid, stat = call(
        functools.partial(middle_kernel, groups),
        [shape((rows, width), BF16)] * 2 + [shape((units, rows), BF16)] * 3 + [shape((8, rows), F32)],
        *across, *mats, *sums, flops=3 * dense // 4, nbytes=3 * units * features // 2,
    )
    rows_in = [rows_local, rows_other, rows_across]
    rows_grad = [grads_local, grads_other, grads_across]

    def input_part(relative, extra, kind):
        return call(
            functools.partial(input_kernel, relative), [shape((rows + extra, width), kind)],
            dgate, dup, mats[0], mats[1], stat, flops=dense // 2, nbytes=units * features,
        )[0]

    far_got = over_expert(input_part(3, EXTRA, BF16), 1)
    far_keep = input_part(2, 0, F32)
    *far_sum, stat_pair = call(
        functools.partial(add_kernel, groups),
        [shape((capacity + EXTRA, width), BF16)] * groups + [shape((8, rows), F32)],
        far_keep, far_got, stat, nbytes=6 * rows * width,
    )
    near_got = over_expert(input_part(1, 0, BF16), 1)
    near_keep = input_part(0, 0, F32)
    crossed = [over_expert(x, 2) for x in far_sum]
    lefts = [(dgate, rows_in), (dup, rows_in), (hid, rows_grad)]
    back, totals, marks = [None] * groups, [None] * groups, [None] * groups
    weight_grads = [None] * 3
    totals[3] = call(functools.partial(join_kernel, 3), [shape((capacity + EXTRA, width), BF16)],
                     near_keep, near_got, crossed[3], stat_pair)[0]
    back[3] = over_node(totals[3], 3)
    weight_grads[0], marks[0] = weight_grad(after((dgate, far_sum[0]))[0], rows_in)
    totals[2] = call(functools.partial(join_kernel, 2), [shape((capacity + EXTRA, width), BF16)],
                     near_keep, near_got, crossed[2], stat_pair, marks[0])[0]
    back[2] = over_node(totals[2], 2)
    totals[1] = call(functools.partial(join_kernel, 1), [shape((capacity + EXTRA, width), BF16)],
                     near_keep, near_got, crossed[1], stat_pair, marks[0])[0]
    back[1] = over_node(totals[1], 1)
    weight_grads[1], marks[1] = weight_grad(after((dup, totals[1], totals[2], totals[3]))[0], rows_in)
    totals[0] = call(functools.partial(join_kernel, 0), [shape((capacity + EXTRA, width), BF16)],
                     near_keep, near_got, crossed[0], stat_pair, marks[1])[0]
    back[0] = totals[0]
    weight_grads[2] = weight_grad(after((hid, back[3]))[0], rows_grad, mark=False)[0]

    grad_in, grad_gates = call(
        functools.partial(finish_kernel, groups),
        [shape((tokens, width), BF16), shape(ids.shape, F32)],
        ids, gates, pick, *back, scratch=[pltpu.VMEM((rows, width), BF16)],
    )
    return (grad_in, grad_gates.T, *weight_grads)


def contract_rows(left, right):
    return lax.dot_general(
        left, right, (((0,), (0,)), ((), ())), preferred_element_type=jnp.float32
    )


def contract_cols(left, right):
    return lax.dot_general(
        left, right, (((1,), (1,)), ((), ())), preferred_element_type=jnp.float32
    )


def expert_backward(rows_in, rows_grad, row_weight, gate_mat, up_mat, down_mat):
    gate_pre = contract_cols(rows_in, gate_mat)
    up_pre = contract_cols(rows_in, up_mat)
    sigmoid_gate = jax.nn.sigmoid(gate_pre)
    silu_gate = gate_pre * sigmoid_gate
    hidden = silu_gate * up_pre
    back_hidden = contract_cols(rows_grad, down_mat)
    statistic = jnp.sum(hidden * back_hidden, axis=1)
    scaled = row_weight[:, None] * back_hidden
    grad_gate_pre = (
        scaled * up_pre * sigmoid_gate * (1.0 + gate_pre * (1.0 - sigmoid_gate))
    ).astype(jnp.bfloat16)
    grad_up_pre = (scaled * silu_gate).astype(jnp.bfloat16)
    weighted_hidden = (row_weight[:, None] * hidden).astype(jnp.bfloat16)
    grad_down = contract_rows(weighted_hidden, rows_grad).astype(jnp.bfloat16)
    grad_gate = contract_rows(grad_gate_pre, rows_in).astype(jnp.bfloat16)
    grad_up = contract_rows(grad_up_pre, rows_in).astype(jnp.bfloat16)
    return (grad_gate, grad_up, grad_down, grad_gate_pre, grad_up_pre, statistic)


def general_local(hidden_in, out_grad, expert_ids, gate_weights, w_gate, w_up, w_down):
    groups = lax.axis_size("node")
    count_tok = hidden_in.shape[0]
    capacity = count_tok // 2
    group_ids = jnp.arange(groups, dtype=jnp.int32)
    member = expert_ids[:, :, None] == group_ids[None, None, :]
    routed = jnp.any(member, axis=1)
    routed_int = routed.astype(jnp.int32)
    position = jnp.cumsum(routed_int, axis=0) - routed_int
    weight_of = jnp.sum(
        jnp.where(member, gate_weights[:, :, None].astype(jnp.float32), jnp.float32(0.0)), axis=1
    )
    slot_ids = jnp.arange(capacity, dtype=jnp.int32)
    landing = routed[:, :, None] & (position[:, :, None] == slot_ids[None, None, :])
    token_of = jnp.sum(
        jnp.where(landing, jnp.arange(count_tok, dtype=jnp.int32)[:, None, None], 0), axis=0
    )
    filled = jnp.any(landing, axis=0)
    send_weight = jnp.where(
        filled, weight_of[token_of, group_ids[:, None]], jnp.float32(0.0)
    ).astype(jnp.bfloat16)

    def pack_rows(source):
        return jnp.where(filled[:, :, None], source[token_of], jnp.zeros((), source.dtype))

    slice_in, slice_grad, recv_weight = (
        lax.all_to_all(pack_rows(hidden_in), "node", split_axis=0, concat_axis=0, tiled=True),
        lax.all_to_all(pack_rows(out_grad), "node", split_axis=0, concat_axis=0, tiled=True),
        lax.all_to_all(send_weight, "node", split_axis=0, concat_axis=0, tiled=True),
    )
    rows_in, rows_grad = (
        lax.all_gather(slice_in, "expert", axis=2, tiled=True),
        lax.all_gather(slice_grad, "expert", axis=2, tiled=True),
    )
    total_rows = groups * capacity
    features = rows_in.shape[2]
    row_weight = recv_weight.reshape(total_rows).astype(jnp.float32)
    gate_mat = w_gate[0]
    up_mat = w_up[0]
    grad_gate, grad_up, grad_down, grad_gate_pre, grad_up_pre, statistic = expert_backward(
        rows_in.reshape(total_rows, features),
        rows_grad.reshape(total_rows, features),
        row_weight,
        gate_mat,
        up_mat,
        w_down[0],
    )
    input_part = jnp.dot(grad_gate_pre, gate_mat, preferred_element_type=jnp.float32) + jnp.dot(
        grad_up_pre, up_mat, preferred_element_type=jnp.float32
    )
    input_slice = lax.psum_scatter(input_part, "expert", scatter_dimension=1, tiled=True)
    stat_total = lax.psum(statistic, "expert")
    slice_width = input_slice.shape[1]
    back_input, back_stat = (
        lax.all_to_all(
            input_slice.reshape(groups, capacity, slice_width),
            "node",
            split_axis=0,
            concat_axis=0,
            tiled=True,
        ),
        lax.all_to_all(
            stat_total.reshape(groups, capacity), "node", split_axis=0, concat_axis=0, tiled=True
        ),
    )
    flat_input = back_input.reshape(total_rows, slice_width)
    flat_stat = back_stat.reshape(total_rows)
    flat_index = expert_ids * capacity + jnp.take_along_axis(position, expert_ids, axis=1)
    grad_in = (flat_input[flat_index[:, 0]] + flat_input[flat_index[:, 1]]).astype(jnp.bfloat16)
    grad_gates = flat_stat[flat_index]
    return (grad_in, grad_gates, grad_gate[None], grad_up[None], grad_down[None])


def local(hidden_in, *rest):
    if (lax.axis_size("node"), lax.axis_size("expert")) == (4, 4) and hidden_in.shape[1] % 128 == 0:
        return fast_local(hidden_in, *rest)
    return general_local(hidden_in, *rest)


def solution(mesh):
    return jax.shard_map(
        local,
        mesh=mesh,
        in_specs=(
            P(("parts", "node"), "expert"),
            P(("parts", "node"), "expert"),
            P(("parts", "node"), None),
            P(("parts", "node"), None),
            P("node", "expert", None),
            P("node", "expert", None),
            P("node", "expert", None),
        ),
        out_specs=(
            P(("parts", "node"), "expert"),
            P(("parts", "node"), None),
            P(("parts", "node"), "expert", None),
            P(("parts", "node"), "expert", None),
            P(("parts", "node"), "expert", None),
        ),
        check_vma=False,
    )
```
